32 devices in a mesh: dp: 8 (over y, x, core), tensor: 4 (over z).
Axes of the slice: x: 2, y: 2, z: 4, core: 2. Of those that a mesh axis runs over, the one named last changes fastest.
Arguments:
- tokens: bfloat16 [16384, 768], P(('dp', 'tensor')), may hold values from -6 to 6
- cotangent: bfloat16 [16384, 768], P(('dp', 'tensor')), may hold values from -6 to 6
- attention_norm_gain: float32 [768], replicated, may hold values from 0.1 to 1.9
- attention_norm_bias: float32 [768], replicated, may hold values from -1.5 to 1.5
- feedforward_norm_gain: float32 [768], replicated, may hold values from 0.1 to 1.9
- feedforward_norm_bias: float32 [768], replicated, may hold values from -1.5 to 1.5
- w_qkv: bfloat16 [768, 3, 768], P(None, None, 'tensor'), may hold values from -0.21875 to 0.21875
- bias_qv: float32 [2, 768], P(None, 'tensor'), may hold values from -2.5 to 2.5
- bias_key: float32 [12, 16], P('tensor'), may hold values from -2.5 to 2.5
- w_dense: bfloat16 [768, 768], P('tensor'), may hold values from -0.875 to 0.875
- bias_dense: float32 [768], replicated, may hold values from -1.5 to 1.5
- w_fc1: bfloat16 [768, 3072], P(None, 'tensor'), may hold values from -0.21875 to 0.21875
- bias_fc1: float32 [3072], P('tensor'), may hold values from -2.5 to 2.5
- w_fc2: bfloat16 [3072, 768], P('tensor'), may hold values from -0.109375 to 0.109375
- bias_fc2: float32 [768], replicated, may hold values from -1.5 to 1.5
Outputs:
- mixed_out: bfloat16 [16384, 768], P(('dp', 'tensor'))
- grad_tokens: bfloat16 [16384, 768], P(('dp', 'tensor'))
- grad_attn_gain: float32 [768], replicated
- grad_attn_shift: float32 [768], replicated
- grad_mlp_gain: float32 [768], replicated
- grad_mlp_shift: float32 [768], replicated
- grad_w_qkv: float32 [768, 3, 768], P(None, None, 'tensor')
- grad_bias_qv: float32 [2, 768], P(None, 'tensor')
- grad_bias_key: float32 [12, 16], P('tensor')
- grad_w_dense: float32 [768, 768], P('tensor')
- grad_bias_dense: float32 [768], replicated
- grad_w_fc1: float32 [768, 3072], P(None, 'tensor')
- grad_bias_fc1: float32 [3072], P('tensor')
- grad_w_fc2: float32 [3072, 768], P('tensor')
- grad_bias_fc2: float32 [768], replicated
The draws below stay inside these ranges and needn't reach their ends.
All inputs are finite; a program needn't handle non-finite values.
Results may differ from the reference program's by a relative error of at most 0.012.
The reference program's roundings to bfloat16 on the way count: a program that leaves them out, or rounds other values in their place, can miss the bound.
Values may be sent and summed in bfloat16 or wider, within the bound.
No kernel may reach another device: no remote copies, remote signals or barrier semaphores. Data moves between devices by JAX's collectives and lax.ppermute only.
A program may use at most 128 MiB of HBM per device.

```python
import jax
import jax.numpy as jnp
from jax import lax

D = 768
H = 12
HD = 64
ROT = 16
FF = 3072
SEQ = 1024
TOKENS = 16384


def levels(stream_key, shape, split, low, largest):
    def one(dim, blocks):
        draws = jax.random.uniform(jax.random.fold_in(jax.random.fold_in(stream_key, 6), dim), (blocks,), jnp.float32, low / len(split), largest / len(split))
        return jnp.repeat(jnp.exp(draws), shape[dim] // blocks).reshape((-1,) + (1,) * (len(shape) - dim - 1))

    factor_of = one(*split[0])
    for cut in split[1:]:
        factor_of = factor_of * one(*cut)
    return factor_of


def scatter_about(stream_key, extent, scale, bound, cuts=(), held_as=jnp.bfloat16):
    factor_of = levels(stream_key, extent, cuts, -0.22, 0.18) if cuts else 1.0
    drawn = jax.random.normal(stream_key, extent, jnp.float32) * scale * factor_of
    return jnp.minimum(jnp.maximum(drawn, -bound), bound).astype(held_as)


def setup_inputs(seed: int = 0) -> dict:
    seeds = jax.random.split(jax.random.key(seed), 16)
    tokens = scatter_about(seeds[0], (TOKENS, D), 1.0, 6.0, ((0, 32),))
    cotangent = scatter_about(seeds[1], (TOKENS, D), 1.0, 6.0, ((0, 32),))
    attention_norm_gain = jnp.clip(1.0 + 0.18 * jax.random.normal(seeds[2], (D,), jnp.float32), 0.1, 1.9)
    attention_norm_bias = scatter_about(seeds[3], (D,), 0.3, 1.5, (), jnp.float32)
    feedforward_norm_gain = jnp.clip(1.0 + 0.18 * jax.random.normal(seeds[4], (D,), jnp.float32), 0.1, 1.9)
    feedforward_norm_bias = scatter_about(seeds[5], (D,), 0.3, 1.5, (), jnp.float32)
    w_qkv = scatter_about(seeds[6], (D, 3, D), D ** -0.5, 0.21875, ((2, 4),))
    bias_qv = scatter_about(seeds[7], (2, D), 0.5, 2.5, ((1, 4),), jnp.float32)
    bias_key = scatter_about(seeds[8], (H, ROT), 0.5, 2.5, ((0, 4),), jnp.float32)
    w_dense = scatter_about(seeds[9], (D, D), (D // 16) ** -0.5, 0.875, ((0, 4),))
    bias_dense = scatter_about(seeds[10], (D,), 0.3, 1.5, (), jnp.float32)
    w_fc1 = scatter_about(seeds[11], (D, FF), D ** -0.5, 0.21875, ((1, 4),))
    bias_fc1 = scatter_about(seeds[12], (FF,), 0.5, 2.5, ((0, 4),), jnp.float32)
    w_fc2 = scatter_about(seeds[13], (FF, D), FF ** -0.5, 0.109375, ((0, 4),))
    bias_fc2 = scatter_about(seeds[14], (D,), 0.3, 1.5, (), jnp.float32)
    return {"tokens": tokens, "cotangent": cotangent, "attention_norm_gain": attention_norm_gain, "attention_norm_bias": attention_norm_bias, "feedforward_norm_gain": feedforward_norm_gain, "feedforward_norm_bias": feedforward_norm_bias, "w_qkv": w_qkv, "bias_qv": bias_qv, "bias_key": bias_key, "w_dense": w_dense, "bias_dense": bias_dense, "w_fc1": w_fc1, "bias_fc1": bias_fc1, "w_fc2": w_fc2, "bias_fc2": bias_fc2}


EPS = 1e-05

@jax.custom_vjp
def low(v):
    return lax.optimization_barrier(v.astype(jnp.bfloat16)).astype(jnp.float32)

@jax.custom_vjp
def low_back(v):
    return v

def low_keep(v):
    return (low(v), None)

def low_pass(kept, grad):
    return (grad,)

def back_keep(v):
    return (v, None)

def back_low(kept, grad):
    return (low(grad),)
low.defvjp(low_keep, low_pass)
low_back.defvjp(back_keep, back_low)

def layer_norm(values, norm_gain_vector, norm_bias_vector):
    row_mean = lax.optimization_barrier(jnp.mean(values, axis=-1, keepdims=True))
    centered_input = values - row_mean
    inverse_deviation = lax.rsqrt(lax.optimization_barrier(jnp.mean(centered_input * centered_input, axis=-1, keepdims=True)) + EPS)
    return centered_input * inverse_deviation * norm_gain_vector + norm_bias_vector

def rotary_tables(row_count, rot_dims):
    position = (jnp.arange(row_count) % SEQ).astype(jnp.float32)
    inverse_deviation = 1.0 / 10000.0 ** (jnp.arange(0, rot_dims, 2).astype(jnp.float32) / rot_dims)
    angles = position[:, None] * inverse_deviation[None, :]
    angles = jnp.concatenate([angles, angles], axis=-1)
    return (jnp.cos(angles)[:, None, :], jnp.sin(angles)[:, None, :])

def turn_half(part, rot_dims):
    half_dims = rot_dims // 2
    return jnp.concatenate([-part[..., half_dims:], part[..., :half_dims]], axis=-1)

def rotate(values, cosine, sine, rot_dims):
    leading = values[..., :rot_dims]
    turned = leading * cosine + turn_half(leading, rot_dims) * sine
    return jnp.concatenate([turned, values[..., rot_dims:]], axis=-1)

def sequence_attention(inputs):
    queries, key_rows, value_rows = inputs
    scores = jnp.einsum('qhd,khd->hqk', queries, key_rows, precision=lax.Precision.HIGHEST) * HD ** (-0.5)
    scores = low_back(scores)
    positions = jnp.arange(SEQ)
    allowed = positions[None, :] <= positions[:, None]
    scores = jnp.where(allowed[None], scores, -1e+30)
    row_max = lax.optimization_barrier(jnp.max(scores, axis=-1, keepdims=True))
    weights = jnp.exp(scores - row_max)
    attn_probs = weights / lax.optimization_barrier(jnp.sum(weights, axis=-1, keepdims=True))
    return jnp.einsum('hqk,khd->qhd', low(attn_probs), value_rows, precision=lax.Precision.HIGHEST)

def layer_forward(tokens_f, attention_norm_gain, attention_norm_bias, feedforward_norm_gain, feedforward_norm_bias, w_qkv, bias_qv, bias_key, w_dense, bias_dense, w_fc1, bias_fc1, w_fc2, bias_fc2):
    row_count = tokens_f.shape[0]
    normalized_first = low(layer_norm(tokens_f, attention_norm_gain, attention_norm_bias))
    normalized_second = low(layer_norm(tokens_f, feedforward_norm_gain, feedforward_norm_bias))
    key_bias = jnp.pad(bias_key, ((0, 0), (0, HD - ROT))).reshape(D)
    bias_all = jnp.concatenate([bias_qv[0], key_bias, bias_qv[1]])
    mixed = jnp.dot(normalized_first, w_qkv.reshape(D, 3 * D), precision=lax.Precision.HIGHEST, preferred_element_type=jnp.float32)
    mixed = low_back(mixed + bias_all).reshape(row_count, 3, H, HD)
    cosine, sine = rotary_tables(row_count, ROT)
    queries = low(rotate(mixed[:, 0], cosine, sine, ROT))
    key_rows = low(rotate(mixed[:, 1], cosine, sine, ROT))
    value_rows = low(mixed[:, 2])
    seq_shape = (row_count // SEQ, SEQ, H, HD)
    attended = lax.map(jax.checkpoint(sequence_attention), (queries.reshape(seq_shape), key_rows.reshape(seq_shape), value_rows.reshape(seq_shape)))
    attended = low(low_back(attended.reshape(row_count, D)))
    attn_out = jnp.dot(attended, w_dense, precision=lax.Precision.HIGHEST, preferred_element_type=jnp.float32)
    hidden = low_back(jnp.dot(normalized_second, w_fc1, precision=lax.Precision.HIGHEST, preferred_element_type=jnp.float32) + bias_fc1)
    activated = low(jax.nn.gelu(hidden, approximate=False))
    mlp_out = jnp.dot(activated, w_fc2, precision=lax.Precision.HIGHEST, preferred_element_type=jnp.float32)
    return tokens_f + attn_out + bias_dense + mlp_out + bias_fc2

def reference(tokens, cotangent, attention_norm_gain, attention_norm_bias, feedforward_norm_gain, feedforward_norm_bias, w_qkv, bias_qv, bias_key, w_dense, bias_dense, w_fc1, bias_fc1, w_fc2, bias_fc2):
    inputs = tuple((array.astype(jnp.float32) for array in (tokens, attention_norm_gain, attention_norm_bias, feedforward_norm_gain, feedforward_norm_bias, w_qkv, bias_qv, bias_key, w_dense, bias_dense, w_fc1, bias_fc1, w_fc2, bias_fc2)))
    result, pullback = jax.vjp(layer_forward, *inputs)
    gradients = pullback(cotangent.astype(jnp.float32))
    return (result.astype(jnp.bfloat16), gradients[0].astype(jnp.bfloat16), gradients[1], gradients[2], gradients[3], gradients[4], gradients[5], gradients[6], gradients[7], gradients[8], gradients[9], gradients[10], gradients[11], gradients[12], gradients[13])
```

```python
import math

import jax
import jax.numpy as jnp
from jax import lax
from jax.experimental import pallas as pl
from jax.experimental.pallas import tpu as pltpu
from jax.sharding import PartitionSpec as P

SEQ = 1024
EPS = 1e-05
BF = jnp.bfloat16
F32 = jnp.float32
BQ = 256
NB = SEQ // BQ
VMEM_LIMIT = 56 * 1024 * 1024


def nn(a, b):
    return lax.dot_general(a, b, (((1,), (0,)), ((), ())), preferred_element_type=F32)


def nt(a, b):
    return lax.dot_general(a, b, (((1,), (1,)), ((), ())), preferred_element_type=F32)


def low_half(shape):
    return lax.broadcasted_iota(jnp.int32, shape, len(shape) - 1) < 64


def spin(u, c, s1, s2):
    return u * c + pltpu.roll(u, 120, 1) * s1 + pltpu.roll(u, 8, 1) * s2


def normalized(x_ref, g_ref, b_ref, n_ref, nt_ref):
    for i in range(NB):
        rows = pl.ds(i * BQ, BQ)
        x = x_ref[rows, :].astype(F32)
        centered = x - jnp.mean(x, axis=-1, keepdims=True)
        r = lax.rsqrt(jnp.mean(centered * centered, axis=-1, keepdims=True) + EPS)
        n = centered * r * g_ref[...] + b_ref[...]
        n_ref[rows, :] = n.astype(BF)
        nt_ref[:, rows] = n.T.astype(BF)


HEADS = ((0, 0, 1, 2, 0), (0, 1, 1, 2, 1), (4, 0, 5, 4, 1))


def tile(i):
    return slice(128 * i, 128 * (i + 1))


def masked(x, half):
    keep = low_half(x.shape)
    zero = jnp.zeros_like(x)
    return jnp.where(keep, x, zero) if half == 0 else jnp.where(keep, zero, x)


def causal(x, fill):
    rows = lax.broadcasted_iota(jnp.int32, x.shape, 0)
    cols = lax.broadcasted_iota(jnp.int32, x.shape, 1)
    return jnp.where(rows <= cols, x, fill)


def attn_forward_kernel(
    x_ref, g_ref, b_ref, w_ref, bias_ref, c_ref, s1_ref, s2_ref,
    n_ref, nt_ref, qkv_ref, lse_ref, ot_ref, out_ref, vt_ref, oacc_ref,
):
    quarter = pl.program_id(0)

    @pl.when(quarter == 0)
    def _():
        normalized(x_ref, g_ref, b_ref, n_ref, nt_ref)

    c, s1, s2 = c_ref[...], s1_ref[...], s2_ref[...]
    low = low_half((SEQ, 128))
    n = n_ref[...]
    scale = 0.125
    m = nn(n, w_ref[0, :, 0:256]) + bias_ref[0, :, 0:256]
    qkv_ref[0, :, tile(0)] = (spin(m[:, :128], c, s1, s2) * scale).astype(BF)
    qkv_ref[0, :, tile(1)] = spin(m[:, 128:], c, s1, s2).astype(BF)
    m = nn(n, w_ref[0, :, tile(2)]) + bias_ref[0, :, tile(2)]
    qkv_ref[0, :, tile(2)] = m.astype(BF)
    qkv_ref[0, :, tile(3)] = jnp.zeros((SEQ, 128), BF)
    vt_ref[0] = m.T.astype(BF)
    m = nn(n, w_ref[0, :, 512:768]) + bias_ref[0, :, 512:768]
    mixed = m[:, :128]
    qkv_ref[0, :, tile(4)] = jnp.where(low, spin(mixed, c, s1, s2) * scale, mixed).astype(BF)
    vt_ref[1] = mixed.T.astype(BF)
    qkv_ref[0, :, tile(5)] = jnp.where(low, spin(m[:, 128:], c, s1, s2), 0.0).astype(BF)

    oacc_ref[pl.ds(128, 64), :] = jnp.zeros((64, SEQ), F32)
    lse_ref[0] = jnp.zeros((8, SEQ), F32)
    for h, (qt, qh, kt, vt, vh) in enumerate(HEADS):
        for j in range(NB):
            cols = pl.ds(j * BQ, BQ)
            past = j * BQ
            q = masked(qkv_ref[0, cols, tile(qt)], qh)
            v_t = vt_ref.at[0 if vt == 2 else 1]
            v_rows = pl.ds(64 * vh, 64)
            st_d = causal(nt(qkv_ref[0, cols, tile(kt)], q), -1e30)
            top = jnp.max(st_d, axis=0, keepdims=True)
            if j:
                st = nt(qkv_ref[0, pl.ds(0, past), tile(kt)], q)
                top = jnp.maximum(top, jnp.max(st, axis=0, keepdims=True))
            w_d = jnp.exp(st_d - top)
            total = jnp.sum(w_d, axis=0, keepdims=True)
            if j:
                w = jnp.exp(st - top)
                total = total + jnp.sum(w, axis=0, keepdims=True)
            inv = 1.0 / total
            o = nn(v_t[v_rows, cols], (w_d * inv).astype(BF))
            if j:
                o = o + nn(v_t[v_rows, pl.ds(0, past)], (w * inv).astype(BF))
            oacc_ref[pl.ds((0, 64, 192)[h], 64), cols] = o
            lse_ref[0, pl.ds(h, 1), cols] = top + jnp.log(total)
    ot = oacc_ref[...]
    ot_ref[0] = ot.astype(BF)
    o = ot.T.astype(BF)
    part = nt(o[:, :128], w_ref[0, :, tile(3)]) + nt(o[:, 128:], w_ref[0, :, tile(5)])

    @pl.when(quarter == 0)
    def _():
        out_ref[...] = part

    @pl.when(quarter != 0)
    def _():
        out_ref[...] += part


def attn_forward(x, gain, shift, wa, bias, tables):
    whole = lambda q: (0, 0)
    per = lambda q: (q, 0, 0)
    return pl.pallas_call(
        attn_forward_kernel,
        grid=(2,),
        in_specs=[
            pl.BlockSpec((SEQ, 768), whole),
            pl.BlockSpec((1, 768), whole),
            pl.BlockSpec((1, 768), whole),
            pl.BlockSpec((1, 768, 768), per),
            pl.BlockSpec((1, 1, 768), per),
            pl.BlockSpec((SEQ, 128), whole),
            pl.BlockSpec((SEQ, 128), whole),
            pl.BlockSpec((SEQ, 128), whole),
        ],
        out_specs=[
            pl.BlockSpec((SEQ, 768), whole),
            pl.BlockSpec((768, SEQ), whole),
            pl.BlockSpec((1, SEQ, 768), per),
            pl.BlockSpec((1, 8, SEQ), per),
            pl.BlockSpec((1, 256, SEQ), per),
            pl.BlockSpec((SEQ, 768), whole),
        ],
        out_shape=[
            jax.ShapeDtypeStruct((SEQ, 768), BF),
            jax.ShapeDtypeStruct((768, SEQ), BF),
            jax.ShapeDtypeStruct((2, SEQ, 768), BF),
            jax.ShapeDtypeStruct((2, 8, SEQ), F32),
            jax.ShapeDtypeStruct((2, 256, SEQ), BF),
            jax.ShapeDtypeStruct((SEQ, 768), F32),
        ],
        scratch_shapes=[pltpu.VMEM((2, 128, SEQ), BF), pltpu.VMEM((256, SEQ), F32)],
        compiler_params=pltpu.CompilerParams(vmem_limit_bytes=VMEM_LIMIT),
        cost_estimate=pl.CostEstimate(flops=8 * 10**9, bytes_accessed=20 * 10**6, transcendentals=4 * 10**6),
        name="attn_forward",
    )(x, gain, shift, wa, bias, *tables)


def gelu_parts(hidden):
    cdf = 0.5 * (1.0 + lax.erf(hidden * math.sqrt(0.5)))
    return cdf


def mlp_forward_kernel(x_ref, g_ref, b_ref, w1_ref, w2_ref, bias_ref, in_ref, n_ref, nt_ref, out_ref):
    first = (pl.program_id(0) == 0) & (pl.program_id(1) == 0)

    @pl.when(first)
    def _():
        normalized(x_ref, g_ref, b_ref, n_ref, nt_ref)
        out_ref[...] = in_ref[...]

    hidden = nn(n_ref[...], w1_ref[0]) + bias_ref[0]
    a = (hidden * gelu_parts(hidden)).astype(BF)
    out_ref[...] += nn(a, w2_ref[0])


def mlp_forward(x, gain, shift, w1, w2, bias, out_in):
    whole = lambda q, j: (0, 0)
    return pl.pallas_call(
        mlp_forward_kernel,
        grid=(2, 3),
        in_specs=[
            pl.BlockSpec((SEQ, 768), whole),
            pl.BlockSpec((1, 768), whole),
            pl.BlockSpec((1, 768), whole),
            pl.BlockSpec((1, 768, 256), lambda q, j: (q, 0, j)),
            pl.BlockSpec((1, 256, 768), lambda q, j: (q, j, 0)),
            pl.BlockSpec((1, 1, 256), lambda q, j: (q, 0, j)),
            pl.BlockSpec((SEQ, 768), whole),
        ],
        out_specs=[
            pl.BlockSpec((SEQ, 768), whole),
            pl.BlockSpec((768, SEQ), whole),
            pl.BlockSpec((SEQ, 768), whole),
        ],
        out_shape=[
            jax.ShapeDtypeStruct((SEQ, 768), BF),
            jax.ShapeDtypeStruct((768, SEQ), BF),
            jax.ShapeDtypeStruct((SEQ, 768), F32),
        ],
        compiler_params=pltpu.CompilerParams(vmem_limit_bytes=VMEM_LIMIT),
        cost_estimate=pl.CostEstimate(flops=5 * 10**9, bytes_accessed=16 * 10**6, transcendentals=2 * 10**6),
        name="mlp_forward",
    )(x, gain, shift, w1, w2, bias, out_in)


def mlp_backward_kernel(n_ref, nt_ref, dy_ref, w1_ref, w2_ref, bias_ref, in_ref, g1_ref, g2_ref, db_ref, dn_ref):
    hidden = nn(n_ref[...], w1_ref[0]) + bias_ref[0]
    cdf = gelu_parts(hidden)
    a_t = (hidden * cdf).T.astype(BF)
    slope = cdf + hidden * (jnp.exp(-0.5 * hidden * hidden) * (1.0 / math.sqrt(2.0 * math.pi)))
    dy = dy_ref[...]
    dh = (nt(dy, w2_ref[0]) * slope).astype(BF)
    g2_ref[...] = nn(a_t, dy)
    g1_ref[...] = nn(nt_ref[...], dh)
    db_ref[...] = jnp.broadcast_to(jnp.sum(dh.astype(F32), axis=0, keepdims=True), (8, 256))
    part = nt(dh, w1_ref[0])

    @pl.when(pl.program_id(0) == 0)
    def _():
        dn_ref[...] = part if in_ref is None else part + in_ref[...]

    @pl.when(pl.program_id(0) != 0)
    def _():
        dn_ref[...] += part


def mlp_backward(quarter, n, n_t, dy, w1, w2, bias, dn_in):
    whole = lambda j: (0, 0)
    in_specs = [
        pl.BlockSpec((SEQ, 768), whole),
        pl.BlockSpec((768, SEQ), whole),
        pl.BlockSpec((SEQ, 768), whole),
        pl.BlockSpec((1, 768, 256), lambda j: (quarter, 0, j)),
        pl.BlockSpec((1, 256, 768), lambda j: (quarter, j, 0)),
        pl.BlockSpec((1, 1, 256), lambda j: (quarter, 0, j)),
    ]
    args = [n, n_t, dy, w1, w2, bias]
    kernel = mlp_backward_kernel
    if dn_in is None:
        kernel = lambda *refs: mlp_backward_kernel(*refs[:6], None, *refs[6:])
    else:
        in_specs.append(pl.BlockSpec((SEQ, 768), whole))
        args.append(dn_in)
    return pl.pallas_call(
        kernel,
        grid=(3,),
        in_specs=in_specs,
        out_specs=[
            pl.BlockSpec((768, 256), lambda j: (0, j)),
            pl.BlockSpec((256, 768), lambda j: (j, 0)),
            pl.BlockSpec((8, 256), lambda j: (0, j)),
            pl.BlockSpec((SEQ, 768), whole),
        ],
        out_shape=[
            jax.ShapeDtypeStruct((768, 768), F32),
            jax.ShapeDtypeStruct((768, 768), F32),
            jax.ShapeDtypeStruct((8, 768), F32),
            jax.ShapeDtypeStruct((SEQ, 768), F32),
        ],
        compiler_params=pltpu.CompilerParams(vmem_limit_bytes=VMEM_LIMIT),
        cost_estimate=pl.CostEstimate(flops=6 * 10**9, bytes_accessed=14 * 10**6, transcendentals=2 * 10**6),
        name="mlp_backward",
    )(*args)


def attn_backward_kernel(
    qkv_ref, lse_ref, ot_ref, nt_ref, dy_ref, w_ref, c_ref, s1_ref, s2_ref, in_ref,
    g_ref, col_ref, dn_ref, do_ref, kt_ref, dk_ref, dv_ref, dqt_ref, d_ref,
):
    c, s1, s2 = c_ref[...], -s1_ref[...], -s2_ref[...]
    low = low_half((SEQ, 128))
    dy = dy_ref[...]
    do_ref[0] = nn(dy, w_ref[0, :, tile(3)]).astype(BF)
    do_ref[1] = nn(dy, w_ref[0, :, tile(5)]).astype(BF)
    kt_ref[0] = qkv_ref[0, :, tile(1)].astype(F32).T.astype(BF)
    kt_ref[1] = qkv_ref[0, :, tile(5)].astype(F32).T.astype(BF)
    dk_ref[...] = jnp.zeros_like(dk_ref)
    dv_ref[...] = jnp.zeros_like(dv_ref)
    for h, (qt, qh, kt, vt, vh) in enumerate(HEADS):
        a = h // 2
        k_rows = pl.ds(64 * qh, 64)
        for j in range(NB):
            cols = pl.ds(j * BQ, BQ)
            past = pl.ds(0, j * BQ)
            q = masked(qkv_ref[0, cols, tile(qt)], qh)
            do = masked(do_ref[a, cols, :], vh)
            lse = lse_ref[0, pl.ds(h, 1), cols]
            p_d = jnp.exp(causal(nt(qkv_ref[0, cols, tile(kt)], q), -1e30) - lse)
            dp_d = nt(qkv_ref[0, cols, tile(vt)], do)
            delta = jnp.sum(p_d * dp_d, axis=0, keepdims=True)
            if j:
                p = jnp.exp(nt(qkv_ref[0, past, tile(kt)], q) - lse)
                dp = nt(qkv_ref[0, past, tile(vt)], do)
                delta = delta + jnp.sum(p * dp, axis=0, keepdims=True)
            ds_d = (p_d * (dp_d - delta)).astype(BF)
            dv_ref[a, cols, :] += nn(p_d.astype(BF), do)
            dk_ref[a, cols, :] += nn(ds_d, q)
            dqt = nn(kt_ref[a, k_rows, cols], ds_d)
            if j:
                ds = (p * (dp - delta)).astype(BF)
                dv_ref[a, past, :] += nn(p.astype(BF), do)
                dk_ref[a, past, :] += nn(ds, q)
                dqt = dqt + nn(kt_ref[a, k_rows, past], ds)
            dqt_ref[a, k_rows, cols] = dqt * 0.125
    dqt_ref[1, pl.ds(64, 64), :] = jnp.zeros((64, SEQ), F32)

    def put(i, value):
        d_ref[:, tile(i)] = value.astype(BF)
        col_ref[:, tile(i)] = jnp.broadcast_to(
            jnp.sum(value.astype(BF).astype(F32), axis=0, keepdims=True), (8, 128)
        )

    put(0, spin(dqt_ref[0].T, c, s1, s2))
    put(1, spin(dk_ref[0], c, s1, s2))
    put(2, dv_ref[0])
    put(3, jnp.zeros((SEQ, 128), F32))
    put(4, jnp.where(low, spin(dqt_ref[1].T, c, s1, s2), dv_ref[1]))
    put(5, jnp.where(low, spin(dk_ref[1], c, s1, s2), 0.0))
    g_ref[...] = nn(nt_ref[...], d_ref[...])
    gd = nn(ot_ref[0], dy)
    g_ref[:, tile(3)] = gd[:128].T
    g_ref[:, tile(5)] += gd[128:].T
    dn = nt(d_ref[...], w_ref[0])
    dn_ref[...] = dn if in_ref is None else dn + in_ref[...]


def attn_backward(quarter, qkv, lse, o_t, n_t, dy, wa, tables, dn_in):
    whole = lambda i: (0, 0)
    per = lambda i: (quarter, 0, 0)
    in_specs = [
        pl.BlockSpec((1, SEQ, 768), per),
        pl.BlockSpec((1, 8, SEQ), per),
        pl.BlockSpec((1, 256, SEQ), per),
        pl.BlockSpec((768, SEQ), whole),
        pl.BlockSpec((SEQ, 768), whole),
        pl.BlockSpec((1, 768, 768), per),
        pl.BlockSpec((SEQ, 128), whole),
        pl.BlockSpec((SEQ, 128), whole),
        pl.BlockSpec((SEQ, 128), whole),
    ]
    args = [qkv, lse, o_t, n_t, dy, wa, *tables]
    kernel = attn_backward_kernel
    if dn_in is None:
        kernel = lambda *refs: attn_backward_kernel(*refs[:9], None, *refs[9:])
    else:
        in_specs.append(pl.BlockSpec((SEQ, 768), whole))
        args.append(dn_in)
    return pl.pallas_call(
        kernel,
        grid=(1,),
        in_specs=in_specs,
        out_specs=[
            pl.BlockSpec((768, 768), whole),
            pl.BlockSpec((8, 768), whole),
            pl.BlockSpec((SEQ, 768), whole),
        ],
        out_shape=[
            jax.ShapeDtypeStruct((768, 768), F32),
            jax.ShapeDtypeStruct((8, 768), F32),
            jax.ShapeDtypeStruct((SEQ, 768), F32),
        ],
        scratch_shapes=[
            pltpu.VMEM((2, SEQ, 128), BF),
            pltpu.VMEM((2, 128, SEQ), BF),
            pltpu.VMEM((2, SEQ, 128), F32),
            pltpu.VMEM((2, SEQ, 128), F32),
            pltpu.VMEM((2, 128, SEQ), F32),
            pltpu.VMEM((SEQ, 768), BF),
        ],
        compiler_params=pltpu.CompilerParams(vmem_limit_bytes=VMEM_LIMIT),
        cost_estimate=pl.CostEstimate(flops=10**10, bytes_accessed=16 * 10**6, transcendentals=2 * 10**6),
        name="attn_backward",
    )(*args)


def swap(value, axis, distance):
    size = lax.axis_size(axis)
    return lax.ppermute(value, axis, [(i, i ^ distance) for i in range(size)])


def bit_of(axis, distance):
    return (lax.axis_index(axis) // distance) % 2


def in_order(bit, own, other, dim=0):
    return jnp.where(bit == 0, jnp.concatenate([own, other], dim), jnp.concatenate([other, own], dim))


def split(value, bit):
    lead, rows, width = value.shape[:-2], value.shape[-2], value.shape[-1]
    pair = value.reshape(*lead, 2, rows // 2, width)
    keep = lax.dynamic_index_in_dim(pair, bit, len(lead), keepdims=False)
    send = lax.dynamic_index_in_dim(pair, 1 - bit, len(lead), keepdims=False)
    return keep, send


def exact(vec):
    high = lax.reduce_precision(vec, 8, 7)
    return jnp.concatenate([high.astype(BF), (vec - high).astype(BF)], 0)


def joined(pair):
    rows = pair.shape[0] // 2
    return pair[:rows].astype(F32) + pair[rows:].astype(F32)


def reduce_step(part, axis, distance, vec=None):
    keep, send = split(part, bit_of(axis, distance))
    if vec is None:
        return keep + swap(send.astype(BF), axis, distance).astype(F32), None
    shape = send.shape
    mine = exact(vec)
    message = jnp.concatenate([send.astype(BF).reshape(-1, shape[-1]), mine], 0)
    got = swap(message, axis, distance)
    rows = message.shape[0] - mine.shape[0]
    return keep + got[:rows].reshape(shape).astype(F32), joined(mine) + joined(got[rows:])


def reduce_block(pair, vec=None):
    both, vec = reduce_step(pair, "dp", 1, vec)
    first, vec = reduce_step(both[0], "dp", 2, vec)
    second, _ = reduce_step(both[1], "dp", 4)
    first, vec = reduce_step(first, "dp", 4, vec)
    second, _ = reduce_step(second, "dp", 2)
    return jnp.stack([first, second]), vec


def gather_block(pair):
    first, second = pair[0], pair[1]
    first = in_order(bit_of("dp", 4), first, swap(first, "dp", 4))
    second = in_order(bit_of("dp", 2), second, swap(second, "dp", 2))
    first = in_order(bit_of("dp", 2), first, swap(first, "dp", 2))
    second = in_order(bit_of("dp", 4), second, swap(second, "dp", 4))
    both = jnp.stack([first, second])
    return in_order(bit_of("dp", 1), both, swap(both, "dp", 1), 1)


def own_piece(pair):
    both, _ = split(pair, bit_of("dp", 1))
    first, _ = split(both[0], bit_of("dp", 2))
    second, _ = split(both[1], bit_of("dp", 4))
    first, _ = split(first, bit_of("dp", 4))
    second, _ = split(second, bit_of("dp", 2))
    return jnp.stack([first, second])


def far_sum(value):
    distance = 8
    while distance < lax.axis_size("dp"):
        mine = lax.reduce_precision(value, 8, 7)
        value = mine + swap(mine.astype(BF), "dp", distance).astype(F32)
        distance *= 2
    return value


def far_sum_exact(vec):
    distance = 8
    while distance < lax.axis_size("dp"):
        mine = exact(vec)
        vec = joined(mine) + joined(swap(mine, "dp", distance))
        distance *= 2
    return vec


def rotary_tables(rot_dims):
    position = jnp.arange(SEQ).astype(F32)
    inverse = 1.0 / 10000.0 ** (jnp.arange(0, rot_dims, 2).astype(F32) / rot_dims)
    angles = position[:, None] * inverse[None, :]
    cosine, sine = jnp.cos(angles), jnp.sin(angles)
    zero = jnp.zeros_like(sine)
    rest = jnp.zeros((SEQ, 64 - rot_dims), F32)
    c = jnp.concatenate([cosine, cosine, rest + 1.0], 1)
    s1 = jnp.concatenate([-sine, zero, rest], 1)
    s2 = jnp.concatenate([zero, sine, rest], 1)
    return tuple(jnp.concatenate([t, t], 1) for t in (c, s1, s2))


def body(
    tokens, cotangent, attention_norm_gain, attention_norm_bias, feedforward_norm_gain, feedforward_norm_bias,
    w_qkv, bias_qv, bias_key, w_dense, bias_dense, w_fc1, bias_fc1, w_fc2, bias_fc2,
):
    rows, width = tokens.shape
    rot_dims = bias_key.shape[1]
    half = bit_of("tensor", 1)

    wq, wk, wv, wd = w_qkv[:, 0], w_qkv[:, 1], w_qkv[:, 2], w_dense.T
    wa_own = jnp.concatenate(
        [wq[:, :128], wk[:, :128], wv[:, :128], wd[:, :128], wq[:, 128:], wv[:, 128:], wk[:, 128:], wd[:, 128:]], 1
    )
    key_bias = jnp.pad(bias_key, ((0, 0), (0, 64 - rot_dims))).reshape(192)
    none = jnp.zeros((128,), F32)
    ba_own = jnp.concatenate(
        [bias_qv[0, :128], key_bias[:128], bias_qv[1, :128], none, bias_qv[0, 128:], bias_qv[1, 128:], key_bias[128:], none[:64]]
    )
    bias_own = jnp.stack([ba_own, bias_fc1])
    wa_halves = wa_own.reshape(2, 384, width)
    pieces = jnp.concatenate(
        [own_piece(jnp.stack([w_fc1, w_fc2])).reshape(192, width), own_piece(wa_halves).reshape(96, width)], 0
    )
    pieces = swap(pieces, "tensor", 2)
    bias_other = swap(bias_own, "tensor", 2)

    tokens_in, cotangent_in, pieces = lax.optimization_barrier((tokens, cotangent, pieces))
    x_far = swap(tokens_in, "tensor", 1)
    cotangent_in, x_far = lax.optimization_barrier((cotangent_in, x_far))
    dy_far = swap(cotangent_in, "tensor", 1)

    fc_piece, a_piece = pieces[:192].reshape(2, 96, width), pieces[192:].reshape(2, 48, width)
    parts = gather_block(jnp.concatenate([fc_piece, a_piece], 1))
    strips = parts.reshape(2, 8, 144, width)
    fc_other = strips[:, :, :96].reshape(2, 768, width)
    wa_other = strips[:, :, 96:].reshape(768, width)
    w1 = jnp.stack([w_fc1, fc_other[0]])
    w2 = jnp.stack([w_fc2, fc_other[1]])
    wa = jnp.stack([wa_own, wa_other])
    bias = jnp.stack([bias_own, bias_other])
    ba, b1 = bias[:, 0:1], bias[:, 1:2]

    tables = rotary_tables(rot_dims)
    x = in_order(half, tokens, x_far)
    dy = in_order(half, cotangent, dy_far)
    gain1, shift1 = attention_norm_gain[None], attention_norm_bias[None]
    gain2, shift2 = feedforward_norm_gain[None], feedforward_norm_bias[None]

    _, n1_t, qkv, lse, o_t, out = attn_forward(x, gain1, shift1, wa, ba, tables)
    n2, n2_t, out = mlp_forward(x, gain2, shift2, w1, w2, b1, out)
    out_keep, out_send = split(out, half)
    out_far = swap(out_send.astype(BF), "tensor", 1).astype(F32)
    own_tokens = tokens.astype(F32)
    mixed_out = (own_tokens + (out_keep + out_far) + bias_dense + bias_fc2).astype(BF)

    g1, g2, db_other, dn2 = mlp_backward(1, n2, n2_t, dy, w1, w2, b1, None)
    fc_far, _ = reduce_block(jnp.stack([g1, g2]))
    fc_far = swap(fc_far.astype(BF), "tensor", 2)
    ga, col_other, dn1 = attn_backward(1, qkv, lse, o_t, n1_t, dy, wa, tables, None)
    a_far, vec_far = reduce_block(ga.reshape(2, 384, width), jnp.stack([db_other[0], col_other[0]]))
    far = jnp.concatenate([a_far.astype(BF).reshape(96, width), exact(vec_far)], 0)
    far = swap(far, "tensor", 2)
    a_far, vec_far = far[:96].reshape(2, 48, width), joined(far[96:])

    g1, g2, db_own, dn2 = mlp_backward(0, n2, n2_t, dy, w1, w2, b1, dn2)
    fc_grad, _ = reduce_block(jnp.stack([g1, g2]))
    fc_grad = far_sum(fc_grad + fc_far.astype(F32))
    fc_grad = gather_block(lax.reduce_precision(fc_grad, 8, 7).astype(BF)).astype(F32)
    ga, col_own, dn1 = attn_backward(0, qkv, lse, o_t, n1_t, dy, wa, tables, dn1)

    e_keep, e_send = split(dn1 * gain1 + dn2 * gain2, half)
    e = e_keep + swap(e_send.astype(BF), "tensor", 1).astype(F32)

    def standardized(value):
        centered = value - jnp.mean(value, axis=-1, keepdims=True)
        r = lax.rsqrt(jnp.mean(centered * centered, axis=-1, keepdims=True) + EPS)
        return centered * r, r

    xhat, r = standardized(own_tokens)
    dx = r * (e - jnp.mean(e, axis=-1, keepdims=True) - xhat * jnp.mean(e * xhat, axis=-1, keepdims=True))
    grad_tokens = (cotangent.astype(F32) + dx).astype(BF)

    xhat_seq, _ = standardized(x.astype(F32))
    vec = jnp.stack(
        [
            db_own[0],
            col_own[0],
            jnp.sum(dn1 * xhat_seq, axis=0),
            jnp.sum(dn1, axis=0),
            jnp.sum(dn2 * xhat_seq, axis=0),
            jnp.sum(dn2, axis=0),
            jnp.sum(cotangent, axis=0, dtype=F32),
        ]
    )
    a_grad, vec = reduce_block(ga.reshape(2, 384, width), vec)
    a_grad = far_sum(a_grad + a_far.astype(F32))
    a_grad = gather_block(lax.reduce_precision(a_grad, 8, 7).astype(BF)).astype(F32).reshape(768, width)
    quarter_vec = far_sum_exact(vec[:2] + vec_far)
    vec = far_sum_exact(vec[2:])
    for distance in (1, 2):
        mine = exact(vec)
        vec = joined(mine) + joined(swap(mine, "tensor", distance))

    def three(values, low, high):
        return jnp.concatenate([values[..., low : low + 128], values[..., high : high + 64]], -1)

    grad_qkv = jnp.stack([three(a_grad, 0, 512), three(a_grad, 128, 640), three(a_grad, 256, 576)], 1)
    grad_dense = three(a_grad, 384, 704).T
    col = quarter_vec[1]
    grad_bias_qv = jnp.stack([three(col, 0, 512), three(col, 256, 576)])
    grad_bias_key = three(col, 128, 640).reshape(3, 64)[:, :rot_dims]
    return (
        mixed_out,
        grad_tokens,
        vec[0],
        vec[1],
        vec[2],
        vec[3],
        grad_qkv,
        grad_bias_qv,
        grad_bias_key,
        grad_dense,
        vec[4],
        fc_grad[0],
        quarter_vec[0],
        fc_grad[1],
        vec[4],
    )


def solution(mesh):
    rows = P(("dp", "tensor"), None)
    in_specs = (
        rows, rows, P(), P(), P(), P(), P(None, None, "tensor"), P(None, "tensor"), P("tensor", None),
        P("tensor", None), P(), P(None, "tensor"), P("tensor"), P("tensor", None), P(),
    )
    out_specs = (
        rows, rows, P(), P(), P(), P(), P(None, None, "tensor"), P(None, "tensor"), P("tensor", None),
        P("tensor", None), P(), P(None, "tensor"), P("tensor"), P("tensor", None), P(),
    )
    return jax.shard_map(body, mesh=mesh, in_specs=in_specs, out_specs=out_specs, check_vma=False)
```

```python
import math

import jax
import jax.numpy as jnp
from jax import lax
from jax.experimental import pallas as pl
from jax.experimental.pallas import tpu as pltpu
from jax.sharding import PartitionSpec as P

SEQ = 1024
EPS = 1e-05
BF = jnp.bfloat16
F32 = jnp.float32
BQ = 256
NB = SEQ // BQ
VMEM_LIMIT = 24 * 1024 * 1024


def nn(a, b):
    return lax.dot_general(a, b, (((1,), (0,)), ((), ())), preferred_element_type=F32)


def nt(a, b):
    return lax.dot_general(a, b, (((1,), (1,)), ((), ())), preferred_element_type=F32)


def call(kernel, name, args, outs, scratch=(), flops=0, transcendentals=0):
    moved = sum(a.size * a.dtype.itemsize for a in args) + sum(math.prod(o[0]) * jnp.dtype(o[1]).itemsize for o in outs)
    spaces = [pltpu.SMEM if a.dtype == jnp.int32 else pltpu.VMEM for a in args]
    args = [pltpu.with_memory_space_constraint(a, pltpu.VMEM) if a.size >= 2**16 else a for a in args]
    return pl.pallas_call(
        kernel,
        in_specs=[pl.BlockSpec(memory_space=s) for s in spaces],
        out_specs=[pl.BlockSpec(memory_space=pltpu.VMEM)] * len(outs),
        out_shape=[pltpu.VMEM(s, d) if stays else jax.ShapeDtypeStruct(s, d) for s, d, stays in outs],
        scratch_shapes=[pltpu.VMEM(s, d) for s, d in scratch],
        compiler_params=pltpu.CompilerParams(vmem_limit_bytes=VMEM_LIMIT),
        cost_estimate=pl.CostEstimate(flops=flops, bytes_accessed=moved, transcendentals=transcendentals),
        name=name,
    )(*args)


def normalized(x_ref, gain, shift, n_ref, nt_ref):
    for i in range(NB):
        rows = pl.ds(i * BQ, BQ)
        x = x_ref[rows, :].astype(F32)
        centered = x - jnp.mean(x, axis=-1, keepdims=True)
        r = lax.rsqrt(jnp.mean(centered * centered, axis=-1, keepdims=True) + EPS)
        n = centered * r * gain + shift
        n_ref[rows, :] = n.astype(BF)
        if nt_ref is not None:
            nt_ref[:, rows] = n.T.astype(BF)


def tile(i):
    return slice(128 * i, 128 * (i + 1))


HEADS = ((0, 0, 1, 2, 0), (0, 1, 1, 2, 1), (4, 0, 5, 4, 1))
TILES = {0: (0, 64), 1: (192, 256), 2: (384, 448), 4: (128, 512), 5: (320, None)}
ROTATED = (0, 64, 128, 192, 256, 320)


def masked(x, half):
    keep = lax.broadcasted_iota(jnp.int32, x.shape, 1) < 64
    zero = jnp.zeros_like(x)
    return jnp.where(keep, x, zero) if half == 0 else jnp.where(keep, zero, x)


def causal(x, fill):
    rows = lax.broadcasted_iota(jnp.int32, x.shape, 0)
    cols = lax.broadcasted_iota(jnp.int32, x.shape, 1)
    return jnp.where(rows <= cols, x, fill)


def attn_forward_kernel(first, *refs):
    if first:
        x_ref, norm_ref, w_ref, bias_ref, cos_ref, sin_ref, n_ref, qkv_ref, kt_ref, lse_ref, ot_ref, out_ref, m_ref, o_ref = refs
        normalized(x_ref, norm_ref[0:1], norm_ref[1:2], n_ref, None)
    else:
        n_ref, w_ref, bias_ref, cos_ref, sin_ref, in_ref, qkv_ref, kt_ref, lse_ref, ot_ref, out_ref, m_ref, o_ref = refs
    n = n_ref[...]
    bias = bias_ref[...].T
    for at, size in ((0, 256), (256, 320)):
        m_ref[pl.ds(at, size), :] = nt(w_ref[pl.ds(at, size), :], n) + bias[at : at + size, 0:1]
    cos, sin = cos_ref[...], sin_ref[...]
    for at in ROTATED:
        one, two = m_ref[pl.ds(at, 8), :], m_ref[pl.ds(at + 8, 8), :]
        m_ref[pl.ds(at, 8), :] = one * cos - two * sin
        m_ref[pl.ds(at + 8, 8), :] = two * cos + one * sin
    m_ref[pl.ds(0, 192), :] = m_ref[pl.ds(0, 192), :] * 0.125
    for i, (one, two) in TILES.items():
        upper = jnp.zeros((64, SEQ), F32) if two is None else m_ref[pl.ds(two, 64), :]
        qkv_ref[:, tile(i)] = jnp.concatenate([m_ref[pl.ds(one, 64), :], upper], 0).T.astype(BF)
    kt_ref[...] = m_ref[pl.ds(192, 192), :].astype(BF)

    lse_ref[...] = jnp.zeros((8, SEQ), F32)
    for h, (qt, qh, kt, vt, vh) in enumerate(HEADS):
        v_rows = pl.ds(384 + 64 * h, 64)
        for j in range(NB):
            cols = pl.ds(j * BQ, BQ)
            past = pl.ds(0, j * BQ)
            q = masked(qkv_ref[cols, tile(qt)], qh)
            st_d = causal(nt(qkv_ref[cols, tile(kt)], q), -1e30)
            top = jnp.max(st_d, axis=0, keepdims=True)
            if j:
                st = nt(qkv_ref[past, tile(kt)], q)
                top = jnp.maximum(top, jnp.max(st, axis=0, keepdims=True))
            w_d = jnp.exp(st_d - top)
            total = jnp.sum(w_d, axis=0, keepdims=True)
            if j:
                w = jnp.exp(st - top)
                total = total + jnp.sum(w, axis=0, keepdims=True)
            inv = 1.0 / total
            o = nn(m_ref[v_rows, cols].astype(BF), (w_d * inv).astype(BF))
            if j:
                o = o + nn(m_ref[v_rows, past].astype(BF), (w * inv).astype(BF))
            o_ref[pl.ds(64 * h, 64), cols] = o
            lse_ref[pl.ds(h, 1), cols] = top + jnp.log(total)
    ot = o_ref[...]
    ot_ref[...] = ot.astype(BF)
    part = nn(ot.T.astype(BF), w_ref[pl.ds(576, 192), :])
    out_ref[...] = part if first else part + in_ref[...]


def attn_forward(x, norm, n, wa, bias, rotary, out_in):
    first = n is None
    args = (x, *norm, wa, bias, *rotary) if first else (n, wa, bias, *rotary, out_in)
    outs = [
        ((SEQ, 768), BF, True),
        ((SEQ, 768), BF, True),
        ((192, SEQ), BF, True),
        ((8, SEQ), F32, False),
        ((192, SEQ), BF, True),
        ((SEQ, 768), F32, True),
    ]
    kernel = lambda *refs: attn_forward_kernel(first, *refs)
    scratch = [((576, SEQ), F32), ((192, SEQ), F32)]
    return call(kernel, "attn_forward", args, outs if first else outs[1:], scratch, 4 * 10**9, 2 * 10**6)


def normal_cdf(hidden):
    return 0.5 * (1.0 + lax.erf(hidden * math.sqrt(0.5)))


def mlp_forward_kernel(first, *refs):
    if first:
        x_ref, norm_ref, w1_ref, w2_ref, bias_ref, in_ref, n_ref, nt_ref, out_ref = refs
        normalized(x_ref, norm_ref[2:3], norm_ref[3:4], n_ref, nt_ref)
    else:
        n_ref, w1_ref, w2_ref, bias_ref, in_ref, out_ref = refs
    for i in range(3):
        cols = slice(256 * i, 256 * (i + 1))
        hidden = nn(n_ref[...], w1_ref[:, cols]) + bias_ref[0:1, cols]
        a = (hidden * normal_cdf(hidden)).astype(BF)
        part = nn(a, w2_ref[cols, :])
        out_ref[...] = part + (in_ref[...] if i == 0 else out_ref[...])


def mlp_forward(x, norm, n, w1, w2, bias, out_in):
    first = n is None
    args = (x, *norm, w1, w2, bias, out_in) if first else (n, w1, w2, bias, out_in)
    outs = [((SEQ, 768), BF, True), ((768, SEQ), BF, True), ((SEQ, 768), F32, True)]
    kernel = lambda *refs: mlp_forward_kernel(first, *refs)
    return call(kernel, "mlp_forward", args, outs if first else outs[2:], (), 25 * 10**8, 10**6)


def mlp_backward_kernel(bits_ref, n_ref, nt_ref, dy_ref, w1_ref, w2_ref, bias_ref, *refs):
    in_ref = refs[0] if len(refs) == 7 else None
    keep_ref, send_ref, db_ref, dn_ref, g1_ref, g2_ref = refs[-6:]
    dy = dy_ref[...]
    for i in range(3):
        cols = slice(256 * i, 256 * (i + 1))
        hidden = nn(n_ref[...], w1_ref[:, cols]) + bias_ref[0:1, cols]
        cdf = normal_cdf(hidden)
        a_t = (hidden * cdf).T.astype(BF)
        slope = cdf + hidden * (jnp.exp(-0.5 * hidden * hidden) * (1.0 / math.sqrt(2.0 * math.pi)))
        dh = (nt(dy, w2_ref[cols, :]) * slope).astype(BF)
        g2_ref[cols, :] = nn(a_t, dy)
        g1_ref[:, cols] = nn(nt_ref[...], dh)
        db_ref[:, cols] = jnp.broadcast_to(jnp.sum(dh.astype(F32), axis=0, keepdims=True), (8, 256))
        part = nt(dh, w1_ref[:, cols])
        if i == 0:
            dn_ref[...] = part if in_ref is None else part + in_ref[...]
        else:
            dn_ref[...] += part
    core = bits_ref[0]
    for i, g in enumerate((g1_ref, g2_ref)):
        keep_ref[i] = g[pl.ds(384 * core, 384), :]
        send_ref[i] = g[pl.ds(384 - 384 * core, 384), :].astype(BF)


def mlp_backward(bits, n, n_t, dy, w1, w2, bias, dn_in):
    args = (bits, n, n_t, dy, w1, w2, bias) + (() if dn_in is None else (dn_in,))
    outs = [((2, 384, 768), F32, True), ((2, 384, 768), BF, False), ((8, 768), F32, False), ((SEQ, 768), F32, True)]
    scratch = [((768, 768), F32)] * 2
    return call(mlp_backward_kernel, "mlp_backward", args, outs, scratch, 6 * 10**9, 2 * 10**6)


def attn_backward_kernel(bits_ref, qkv_ref, kt_ref, lse_ref, ot_ref, n_ref, dy_ref, w_ref, cos_ref, sin_ref, db_ref, *refs):
    last = len(refs) == 14
    if last:
        in_ref, dn2_ref, x_ref, gains_ref, keep_ref, send_ref, e_keep_ref, e_send_ref = refs[:8]
    else:
        keep_ref, send_ref, dn_ref = refs[:3]
    do_ref, dk_ref, dv_ref, dt_ref, d_ref, g_ref = refs[-6:]
    dy = dy_ref[...]
    do_ref[0] = nt(dy, w_ref[pl.ds(576, 128), :]).astype(BF)
    do_ref[1] = nt(dy, w_ref[pl.ds(640, 128), :]).astype(BF)
    dk_ref[...] = jnp.zeros_like(dk_ref)
    dv_ref[...] = jnp.zeros_like(dv_ref)
    for h, (qt, qh, kt, vt, vh) in enumerate(HEADS):
        a = h // 2
        rows = pl.ds(64 * h, 64)
        for j in range(NB):
            cols = pl.ds(j * BQ, BQ)
            past = pl.ds(0, j * BQ)
            q = masked(qkv_ref[cols, tile(qt)], qh)
            do = masked(do_ref[a, cols, :], vh)
            lse = lse_ref[pl.ds(h, 1), cols]
            p_d = jnp.exp(causal(nt(qkv_ref[cols, tile(kt)], q), -1e30) - lse)
            dp_d = nt(qkv_ref[cols, tile(vt)], do)
            delta = jnp.sum(p_d * dp_d, axis=0, keepdims=True)
            if j:
                p = jnp.exp(nt(qkv_ref[past, tile(kt)], q) - lse)
                dp = nt(qkv_ref[past, tile(vt)], do)
                delta = delta + jnp.sum(p * dp, axis=0, keepdims=True)
            ds_d = (p_d * (dp_d - delta)).astype(BF)
            dv_ref[a, cols, :] += nn(p_d.astype(BF), do)
            dk_ref[a, cols, :] += nn(ds_d, q)
            dqt = nn(kt_ref[rows, cols], ds_d)
            if j:
                ds = (p * (dp - delta)).astype(BF)
                dv_ref[a, past, :] += nn(p.astype(BF), do)
                dk_ref[a, past, :] += nn(ds, q)
                dqt = dqt + nn(kt_ref[rows, past], ds)
            dt_ref[rows, cols] = dqt * 0.125
    dt_ref[pl.ds(192, 128), :] = dk_ref[0].T
    dt_ref[pl.ds(320, 64), :] = dk_ref[1].T[:64]
    dt_ref[pl.ds(384, 128), :] = dv_ref[0].T
    dt_ref[pl.ds(512, 64), :] = dv_ref[1].T[64:]
    dt_ref[pl.ds(576, 64), :] = jnp.zeros((64, SEQ), F32)
    cos, sin = cos_ref[...], sin_ref[...]
    for at in ROTATED:
        one, two = dt_ref[pl.ds(at, 8), :], dt_ref[pl.ds(at + 8, 8), :]
        dt_ref[pl.ds(at, 8), :] = one * cos + two * sin
        dt_ref[pl.ds(at + 8, 8), :] = two * cos - one * sin
    for i in range(5):
        d_ref[:, tile(i)] = dt_ref[tile(i), :].T.astype(BF)
    d = d_ref[...]
    g_ref[pl.ds(0, 576), :] = nn(dt_ref[pl.ds(0, 576), :].astype(BF), n_ref[...])
    g_ref[pl.ds(576, 192), :] = nn(ot_ref[...], dy)
    dn = nn(d, w_ref[pl.ds(0, 640), :])

    core = bits_ref[0]
    keep_ref[...] = g_ref[pl.ds(384 * core, 384), :]
    send_ref[pl.ds(0, 384), :] = g_ref[pl.ds(384 - 384 * core, 384), :].astype(BF)
    row = lax.broadcasted_iota(jnp.int32, (8, 768), 0)
    columns = jnp.concatenate([nn(jnp.ones((8, SEQ), BF), d), jnp.zeros((8, 128), F32)], 1)
    vec = jnp.where(row == 0, db_ref[...], jnp.where(row == 1, columns, 0.0))
    if last:
        half = bits_ref[1]
        dn2, gains = dn2_ref[...], gains_ref[...]
        dn = dn + in_ref[...]
        e = dn * gains[0:1] + dn2 * gains[2:3]
        x = x_ref[...].astype(F32)
        centered = x - jnp.mean(x, axis=-1, keepdims=True)
        xhat = centered * lax.rsqrt(jnp.mean(centered * centered, axis=-1, keepdims=True) + EPS)
        sums = (
            jnp.sum(dn * xhat, axis=0, keepdims=True),
            jnp.sum(dn, axis=0, keepdims=True),
            jnp.sum(dn2 * xhat, axis=0, keepdims=True),
            jnp.sum(dn2, axis=0, keepdims=True),
            jnp.sum(dy_ref[pl.ds(512 * half, 512), :].astype(F32), axis=0, keepdims=True),
        )
        for i, value in enumerate(sums):
            vec = jnp.where(row == 2 + i, value, vec)
        e_low, e_high = e[:512], e[512:]

        @pl.when(half == 0)
        def _():
            e_keep_ref[...] = e_low
            e_send_ref[...] = e_high.astype(BF)

        @pl.when(half != 0)
        def _():
            e_keep_ref[...] = e_high
            e_send_ref[...] = e_low.astype(BF)
    else:
        dn_ref[...] = dn
    high = vec.astype(BF)
    send_ref[pl.ds(384, 16), :] = jnp.concatenate([high, (vec - high.astype(F32)).astype(BF)], 0)


def attn_backward(bits, saved, n, dy, wa, rotary, db, more):
    args = (bits, *saved, n, dy, wa, *rotary, db, *more)
    outs = [((384, 768), F32, True), ((400, 768), BF, False)]
    if more:
        outs += [((512, 768), F32, True), ((512, 768), BF, False)]
    else:
        outs += [((SEQ, 768), F32, True)]
    scratch = [
        ((2, SEQ, 128), BF),
        ((2, SEQ, 128), F32),
        ((2, SEQ, 128), F32),
        ((640, SEQ), F32),
        ((SEQ, 640), BF),
        ((768, 768), F32),
    ]
    return call(attn_backward_kernel, "attn_backward", args, outs, scratch, 5 * 10**9, 10**6)


def swap(value, axis, distance):
    size = lax.axis_size(axis)
    return lax.ppermute(value, axis, [(i, i ^ distance) for i in range(size)])


def bit_of(axis, distance):
    return (lax.axis_index(axis) // distance) % 2


def in_order(bit, own, other, dim=0):
    return jnp.where(bit == 0, jnp.concatenate([own, other], dim), jnp.concatenate([other, own], dim))


def split(value, bit):
    rows = value.shape[0] // 2
    keep = lax.dynamic_slice_in_dim(value, bit * rows, rows, 0)
    return keep, lax.dynamic_slice_in_dim(value, (1 - bit) * rows, rows, 0)


def exact(vec):
    high = lax.reduce_precision(vec, 8, 7)
    return jnp.concatenate([high.astype(BF), (vec - high).astype(BF)], 0)


def joined(pair):
    rows = pair.shape[0] // 2
    return pair[:rows].astype(F32) + pair[rows:].astype(F32)


def spot():
    return 2 * bit_of("dp", 2) + bit_of("dp", 4)


PEERS = ((4, 1), (2, 2), (6, 3))


def messages(keep, got, vec=None):
    def part(change):
        at = (spot() ^ change) * 96
        cut = lambda v: lax.dynamic_slice_in_dim(v, at, 96, 1)
        return cut(keep) + cut(got).astype(F32)

    out = []
    for _, change in PEERS:
        sent = part(change).astype(BF).reshape(-1, keep.shape[-1])
        out.append(sent if vec is None else jnp.concatenate([sent, exact(vec)], 0))
    return part(0), out


def exchange(out):
    return [swap(message, "dp", distance) for (distance, _), message in zip(PEERS, out)]


def summed(own, got, vec=None):
    rows = own.shape[0] * 96
    total = own
    for message in got:
        total = total + message[:rows].reshape(own.shape).astype(F32)
    if vec is None:
        return total
    y, x, both = (joined(message[rows:]) for message in got)
    return total, (joined(exact(vec)) + y) + (x + both)


def arranged(own, got):
    y, x, both = (message.reshape(own.shape) for message in got)
    low = in_order(bit_of("dp", 4), own, y, 1)
    high = in_order(bit_of("dp", 4), x, both, 1)
    return in_order(bit_of("dp", 2), low, high, 1)


def far_sum(value):
    distance = 8
    while distance < lax.axis_size("dp"):
        mine = lax.reduce_precision(value, 8, 7)
        value = mine + swap(mine.astype(BF), "dp", distance).astype(F32)
        distance *= 2
    return value


def far_sum_exact(vec):
    distance = 8
    while distance < lax.axis_size("dp"):
        mine = exact(vec)
        vec = joined(mine) + joined(swap(mine, "dp", distance))
        distance *= 2
    return vec


def rotary_tables(rot_dims):
    position = jnp.arange(SEQ).astype(F32)
    inverse = 1.0 / 10000.0 ** (jnp.arange(0, rot_dims, 2).astype(F32) / rot_dims)
    angles = inverse[:, None] * position[None, :]
    return jnp.cos(angles), jnp.sin(angles)


def tied(values, *others):
    return lax.optimization_barrier((values, others))[0]


def body(
    tokens, cotangent, attention_norm_gain, attention_norm_bias, feedforward_norm_gain, feedforward_norm_bias,
    w_qkv, bias_qv, bias_key, w_dense, bias_dense, w_fc1, bias_fc1, w_fc2, bias_fc2,
):
    width = tokens.shape[1]
    rot_dims = bias_key.shape[1]
    half, core = bit_of("tensor", 1), bit_of("dp", 1)
    bits = jnp.stack([core, half]).astype(jnp.int32)

    x_far = swap(tokens, "tensor", 1)

    wa_own = jnp.concatenate([w_qkv.transpose(1, 2, 0).reshape(-1, width), w_dense], 0)
    key_bias = jnp.pad(bias_key, ((0, 0), (0, 64 - rot_dims))).reshape(192)
    bias_own = jnp.stack([jnp.concatenate([bias_qv[0], key_bias, bias_qv[1], jnp.zeros((192,), F32)]), bias_fc1])
    at = (4 * core + spot()) * 96
    pieces = jnp.stack([lax.dynamic_slice_in_dim(w, at, 96, 0) for w in (w_fc1, w_fc2, wa_own)])
    far_pieces = swap(pieces, "tensor", 2)
    bias_other = swap(bias_own, "tensor", 2)
    dy_far = swap(tied(cotangent, x_far), "tensor", 1)

    rotary = rotary_tables(rot_dims)
    pad8 = lambda row: jnp.broadcast_to(row[None], (8, width))
    ba_own, b1_own = pad8(bias_own[0]), pad8(bias_own[1])
    ba_other, b1_other = pad8(bias_other[0]), pad8(bias_other[1])
    x = in_order(half, tokens, x_far)
    norms = jnp.stack([attention_norm_gain, attention_norm_bias, feedforward_norm_gain, feedforward_norm_bias])

    n1, *saved_own, out = attn_forward(tied(x, pieces), (norms,), None, wa_own, ba_own, rotary, None)
    out, far_pieces, dy_far = tied((out, far_pieces, dy_far), far_pieces, dy_far)
    got = exchange([far_pieces.reshape(288, width)] * 3)
    n2, n2_t, out = mlp_forward(x, (norms,), None, w_fc1, w_fc2, b1_own, out)
    dy = in_order(half, cotangent, dy_far)
    keep, send, db_own, dn2 = mlp_backward(bits, n2, n2_t, dy, w_fc1, w_fc2, b1_own, None)
    keep, send, dn2, out, got = tied((keep, send, dn2, out, got), got)
    parts = arranged(far_pieces, got)
    parts_far, send_far = swap(parts, "dp", 1), swap(send, "dp", 1)
    w1_other, w2_other, wa_other = (in_order(core, parts[i], parts_far[i]) for i in range(3))

    fc_own, sent = messages(keep, send_far)
    got = exchange(sent)
    out = mlp_forward(None, None, n2, w1_other, w2_other, b1_other, tied(out, sent))[0]
    keep, send, db_other, dn2 = mlp_backward(bits, n2, n2_t, dy, w1_other, w2_other, b1_other, tied(dn2, out))
    out, keep, send, got = tied((out, keep, send, got), got)
    fc_own = summed(fc_own, got)

    send_far = swap(send, "dp", 1)
    *saved, out = attn_forward(None, None, n1, wa_other, ba_other, rotary, tied(out, fc_own))
    out, saved, send_far = tied((out, saved, send_far), send_far)
    out_keep, out_send = split(out, half)
    out_send = out_send.astype(BF)
    out_far = swap(out_send, "tensor", 1)
    fc_far, sent = messages(keep, send_far)
    got = exchange(sent)
    keep, send, dn1 = attn_backward(bits, tied(saved, out_send, sent), n1, dy, wa_other, rotary, db_other, ())
    keep, send, dn1, out_far, got = tied((keep, send, dn1, out_far, got), out_far, got)
    own_tokens = tokens.astype(F32)
    mixed_out = (own_tokens + (out_keep + out_far.astype(F32)) + bias_dense + bias_fc2).astype(BF)

    fc_far = summed(fc_far, got).astype(BF)
    fc_far = swap(fc_far, "tensor", 2)
    send_far = swap(send, "dp", 1)
    vec_far = joined(send[384:]) + joined(send_far[384:])
    a_far, sent = messages(keep[None], send_far[None, :384], vec_far)
    got = exchange(sent)
    keep, send, e_keep, e_send = attn_backward(
        bits, saved_own, n1, dy, wa_own, rotary, db_own, (tied(dn1, sent, mixed_out), dn2, x, norms)
    )
    keep, send, e_keep, e_send, got, fc_far = tied((keep, send, e_keep, e_send, got, fc_far), got, fc_far)

    send_far = swap(send, "dp", 1)
    e_far = swap(e_send, "tensor", 1)
    a_far, vec_far = summed(a_far, got, vec_far)
    far = swap(jnp.concatenate([a_far[0].astype(BF), exact(vec_far)], 0), "tensor", 2)
    fc_grad = lax.reduce_precision(far_sum(fc_own + fc_far.astype(F32)), 8, 7).astype(BF)
    fc_got = exchange([fc_grad.reshape(192, width)] * 3)
    vec = joined(send[384:]) + joined(send_far[384:])
    a_own, sent = messages(keep[None], send_far[None, :384], vec)
    got = exchange(sent)
    a_own, vec = summed(a_own, got, vec)
    a_grad = far_sum(a_own + far[None, :96].astype(F32))
    a_grad = lax.reduce_precision(a_grad, 8, 7).astype(BF)
    a_got = exchange([a_grad.reshape(96, width)] * 3)
    quarter_vec = far_sum_exact(vec + joined(far[96:]))
    vec = far_sum_exact(vec)
    for distance in (1, 2):
        mine = exact(vec)
        vec = joined(mine) + joined(swap(mine, "tensor", distance))
    grads = jnp.concatenate([arranged(fc_grad, fc_got), arranged(a_grad, a_got)], 0)
    grads_far = swap(grads, "dp", 1)
    fc1_grad, fc2_grad, a_grad = (in_order(core, grads[i], grads_far[i]).astype(F32) for i in range(3))

    e = e_keep + e_far.astype(F32)
    centered = own_tokens - jnp.mean(own_tokens, axis=-1, keepdims=True)
    r = lax.rsqrt(jnp.mean(centered * centered, axis=-1, keepdims=True) + EPS)
    xhat = centered * r
    dx = r * (e - jnp.mean(e, axis=-1, keepdims=True) - xhat * jnp.mean(e * xhat, axis=-1, keepdims=True))
    grad_tokens = (cotangent.astype(F32) + dx).astype(BF)

    columns = quarter_vec[1]
    return (
        mixed_out,
        grad_tokens,
        vec[2],
        vec[3],
        vec[4],
        vec[5],
        a_grad[:576].reshape(3, 192, width).transpose(2, 0, 1),
        jnp.stack([columns[:192], columns[384:576]]),
        columns[192:384].reshape(3, 64)[:, :rot_dims],
        a_grad[576:],
        vec[6],
        fc1_grad,
        quarter_vec[0],
        fc2_grad,
        vec[6],
    )


def solution(mesh):
    rows = P(("dp", "tensor"), None)
    in_specs = (
        rows, rows, P(), P(), P(), P(), P(None, None, "tensor"), P(None, "tensor"), P("tensor", None),
        P("tensor", None), P(), P(None, "tensor"), P("tensor"), P("tensor", None), P(),
    )
    out_specs = (
        rows, rows, P(), P(), P(), P(), P(None, None, "tensor"), P(None, "tensor"), P("tensor", None),
        P("tensor", None), P(), P(None, "tensor"), P("tensor"), P("tensor", None), P(),
    )
    return jax.shard_map(body, mesh=mesh, in_specs=in_specs, out_specs=out_specs, check_vma=False)
```

```python
import math

import jax
import jax.numpy as jnp
from jax import lax
from jax.experimental import pallas as pl
from jax.experimental.pallas import tpu as pltpu
from jax.sharding import PartitionSpec as P

SEQ = 1024
EPS = 1e-05
BF = jnp.bfloat16
F32 = jnp.float32
BQ = 256
NB = SEQ // BQ
HALF = SEQ // 2


def nn(a, b):
    return lax.dot_general(a, b, (((1,), (0,)), ((), ())), preferred_element_type=F32)


def nt(a, b):
    return lax.dot_general(a, b, (((1,), (1,)), ((), ())), preferred_element_type=F32)


def call(kernel, name, args, outs, scratch=(), flops=0, transcendentals=0, limit=28):
    moved = sum(a.size * a.dtype.itemsize for a in args) + sum(math.prod(o[0]) * jnp.dtype(o[1]).itemsize for o in outs)
    spaces = [pltpu.SMEM if a.dtype == jnp.int32 else pltpu.VMEM for a in args]
    return pl.pallas_call(
        kernel,
        in_specs=[pl.BlockSpec(memory_space=s) for s in spaces],
        out_specs=[pl.BlockSpec(memory_space=pltpu.VMEM)] * len(outs),
        out_shape=[(pltpu.VMEM if stays else pltpu.HBM)(s, d) for s, d, stays in outs],
        scratch_shapes=[pltpu.VMEM(s, d) for s, d in scratch],
        compiler_params=pltpu.CompilerParams(vmem_limit_bytes=limit * 2**20),
        cost_estimate=pl.CostEstimate(flops=flops, bytes_accessed=moved, transcendentals=transcendentals),
        name=name,
    )(*args)


def near(values):
    return jax.tree.map(lambda v: pltpu.with_memory_space_constraint(v, pltpu.VMEM), values)


def away(values):
    return jax.tree.map(lambda v: pltpu.with_memory_space_constraint(v, pltpu.HBM), values)


def own_rows(bits_ref):
    half = bits_ref[1]
    return pl.ds(pl.multiple_of(HALF * half, HALF), HALF), pl.ds(pl.multiple_of(HALF - HALF * half, HALF), HALF)


def place_strips(bits_ref, mine, theirs, put):
    for slot in range(4):
        at = 96 * (bits_ref[2] ^ slot)
        put(pl.multiple_of(384 * bits_ref[0] + at, 96), mine[slot])
        put(pl.multiple_of(384 - 384 * bits_ref[0] + at, 96), theirs[slot])


def normalized(x_ref, gain, shift, put):
    for i in range(HALF // BQ):
        rows = pl.ds(i * BQ, BQ)
        x = x_ref[rows, :].astype(F32)
        centered = x - jnp.mean(x, axis=-1, keepdims=True)
        r = lax.rsqrt(jnp.mean(centered * centered, axis=-1, keepdims=True) + EPS)
        put(i * BQ, centered * r * gain + shift)


def tile(i):
    return slice(128 * i, 128 * (i + 1))


HEADS = ((0, 0, 1, 2, 0), (0, 1, 1, 2, 1), (4, 0, 5, 4, 1))
TILES = {0: (0, 64), 1: (192, 256), 2: (384, 448), 4: (128, 512), 5: (320, None)}
ROTATED = (0, 64, 128, 192, 256, 320)


def masked(x, half):
    keep = lax.broadcasted_iota(jnp.int32, x.shape, 1) < 64
    zero = jnp.zeros_like(x)
    return jnp.where(keep, x, zero) if half == 0 else jnp.where(keep, zero, x)


def causal(x, fill):
    rows = lax.broadcasted_iota(jnp.int32, x.shape, 0)
    cols = lax.broadcasted_iota(jnp.int32, x.shape, 1)
    return jnp.where(rows <= cols, x, fill)


def attn_forward_kernel(first, *refs):
    if first:
        bits_ref, x_ref, x_far_ref, norm_ref, w_ref, bias_ref, cos_ref, sin_ref = refs[:8]
        n_ref, qkv_ref, kt_ref, lse_ref, ot_ref, m_ref, o_ref = refs[8:]
        for x, at in ((x_ref, HALF * bits_ref[1]), (x_far_ref, HALF - HALF * bits_ref[1])):
            def put(row, n):
                n_ref[pl.ds(pl.multiple_of(at + row, BQ), BQ), :] = n.astype(BF)

            normalized(x, norm_ref[0:1], norm_ref[1:2], put)
    else:
        bits_ref, n_ref, w_ref, bias_ref, cos_ref, sin_ref, ot_in_ref, wd_in_ref, mlp_ref, mlp_far_ref = refs[:10]
        qkv_ref, kt_ref, lse_ref, ot_ref, keep_ref, send_ref, m_ref, o_ref, out_ref = refs[10:]
    n = n_ref[...]
    bias = bias_ref[...].T
    for at, size in ((0, 256), (256, 320)):
        m_ref[pl.ds(at, size), :] = nt(w_ref[pl.ds(at, size), :], n) + bias[at : at + size, 0:1]
    cos, sin = cos_ref[...], sin_ref[...]
    for at in ROTATED:
        one, two = m_ref[pl.ds(at, 8), :], m_ref[pl.ds(at + 8, 8), :]
        m_ref[pl.ds(at, 8), :] = one * cos - two * sin
        m_ref[pl.ds(at + 8, 8), :] = two * cos + one * sin
    m_ref[pl.ds(0, 192), :] = m_ref[pl.ds(0, 192), :] * 0.125
    for i, (one, two) in TILES.items():
        upper = jnp.zeros((64, SEQ), F32) if two is None else m_ref[pl.ds(two, 64), :]
        qkv_ref[:, tile(i)] = jnp.concatenate([m_ref[pl.ds(one, 64), :], upper], 0).T.astype(BF)
    kt_ref[...] = m_ref[pl.ds(192, 192), :].astype(BF)

    lse_ref[...] = jnp.zeros((8, SEQ), F32)
    for h, (qt, qh, kt, vt, vh) in enumerate(HEADS):
        v_rows = pl.ds(384 + 64 * h, 64)
        for j in range(NB):
            cols = pl.ds(j * BQ, BQ)
            past = pl.ds(0, j * BQ)
            q = masked(qkv_ref[cols, tile(qt)], qh)
            st_d = causal(nt(qkv_ref[cols, tile(kt)], q), -1e30)
            top = jnp.max(st_d, axis=0, keepdims=True)
            if j:
                st = nt(qkv_ref[past, tile(kt)], q)
                top = jnp.maximum(top, jnp.max(st, axis=0, keepdims=True))
            w_d = jnp.exp(st_d - top)
            total = jnp.sum(w_d, axis=0, keepdims=True)
            if j:
                w = jnp.exp(st - top)
                total = total + jnp.sum(w, axis=0, keepdims=True)
            inv = 1.0 / total
            o = nn(m_ref[v_rows, cols].astype(BF), (w_d * inv).astype(BF))
            if j:
                o = o + nn(m_ref[v_rows, past].astype(BF), (w * inv).astype(BF))
            o_ref[pl.ds(64 * h, 64), cols] = o
            lse_ref[pl.ds(h, 1), cols] = top + jnp.log(total)
    ot_ref[...] = o_ref[...].astype(BF)
    if not first:
        own, far = own_rows(bits_ref)
        out_ref[...] = nn(o_ref[...].T.astype(BF), w_ref[pl.ds(576, 192), :]) + nn(
            ot_in_ref[...].astype(F32).T.astype(BF), wd_in_ref[...]
        )
        keep_ref[...] = out_ref[own, :] + mlp_ref[...].astype(F32)
        send_ref[...] = (out_ref[far, :] + mlp_far_ref[...].astype(F32)).astype(BF)


def attn_forward(first, *args):
    outs = [
        ((SEQ, 768), BF, False),
        ((SEQ, 768), BF, not first),
        ((192, SEQ), BF, not first),
        ((8, SEQ), F32, False),
        ((192, SEQ), BF, not first),
    ]
    scratch = [((576, SEQ), F32), ((192, SEQ), F32)]
    if not first:
        outs = outs[1:] + [((HALF, 768), F32, False), ((HALF, 768), BF, False)]
        scratch.append(((SEQ, 768), F32))
    kernel = lambda *refs: attn_forward_kernel(first, *refs)
    return call(kernel, "attn_forward", args, outs, scratch, 4 * 10**9, 2 * 10**6)


def normal_cdf(hidden):
    return 0.5 * (1.0 + lax.erf(hidden * math.sqrt(0.5)))


def mlp_block(i, n_ref, nt_ref, dy_ref, w1_ref, w2_ref, bias_ref):
    cols = slice(256 * i, 256 * (i + 1))
    w1, w2, dy = w1_ref[:, cols], w2_ref[cols, :], dy_ref[...]
    hidden = nn(n_ref[...], w1) + bias_ref[0:1, cols]
    cdf = normal_cdf(hidden)
    a = (hidden * cdf).astype(BF)
    slope = cdf + hidden * (jnp.exp(-0.5 * hidden * hidden) * (1.0 / math.sqrt(2.0 * math.pi)))
    dh = (nt(dy, w2) * slope).astype(BF)
    db = jnp.broadcast_to(jnp.sum(dh.astype(F32), axis=0, keepdims=True), (8, 256))
    return nn(a, w2), nt(dh, w1), nn(nt_ref[...], dh), nn(a.T, dy), db


def add(i, ref, value):
    if i:
        ref[...] += value
    else:
        ref[...] = value


def split_gradients(bits_ref, grads, keep_ref, send_ref):
    core = bits_ref[0]
    for i, g in enumerate(grads):
        keep_ref[i] = g[pl.ds(pl.multiple_of(384 * core, 384), 384), :].astype(BF)
        send_ref[i] = g[pl.ds(pl.multiple_of(384 - 384 * core, 384), 384), :].astype(BF)


def second_norm(x_ref, norm_ref, n_ref, nt_ref):
    def put(row, n):
        n_ref[pl.ds(row, BQ), :] = n.astype(BF)
        nt_ref[:, pl.ds(row, BQ)] = n.T.astype(BF)

    normalized(x_ref, norm_ref[2:3], norm_ref[3:4], put)


def mlp_half_kernel(first, *refs):
    if first:
        x_ref, norm_ref, dy_ref, w1_ref, w2_ref, bias_ref = refs[:6]
        out_low_ref, dn_low_ref, db_ref, g1_ref, g2_ref, n_ref, nt_ref, out_ref, dn_ref = refs[6:]
    else:
        x_ref, norm_ref, dy_ref, w1_ref, w2_ref, bias_ref, bits_ref, db_in_ref, g1_in_ref, g2_in_ref = refs[:10]
        out_low_ref, dn_low_ref, db_ref, keep_ref, send_ref, n_ref, nt_ref, out_ref, dn_ref, g1_ref, g2_ref = refs[10:]
    second_norm(x_ref, norm_ref, n_ref, nt_ref)
    for i in range(3):
        cols = slice(256 * i, 256 * (i + 1))
        out, dn, g1, g2, db = mlp_block(i, n_ref, nt_ref, dy_ref, w1_ref, w2_ref, bias_ref)
        add(i, out_ref, out)
        add(i, dn_ref, dn)
        g1_ref[:, cols] = g1 if first else g1 + g1_in_ref[:, cols]
        g2_ref[cols, :] = g2 if first else g2 + g2_in_ref[cols, :]
        db_ref[:, cols] = db if first else db + db_in_ref[:, cols]
    out_low_ref[...] = out_ref[...].astype(BF)
    dn_low_ref[...] = dn_ref[...].astype(BF)
    if not first:
        split_gradients(bits_ref, (g1_ref, g2_ref), keep_ref, send_ref)


NORMED = [((HALF, 768), BF), ((768, HALF), BF)]
SUMS = [((HALF, 768), F32)] * 2
SPLIT_OUTS = [((2, 384, 768), BF, False)] * 2


def mlp_half(first, *args):
    grads = [((768, 768), F32, True)] * 2
    outs = [((HALF, 768), BF, False)] * 2 + [((8, 768), F32, False)] + (grads if first else SPLIT_OUTS)
    scratch = NORMED + SUMS + ([] if first else [g[:2] for g in grads])
    kernel = lambda *refs: mlp_half_kernel(first, *refs)
    return call(kernel, "mlp_half", args, outs, scratch, 36 * 10**8, 10**6)


def mlp_other_kernel(*refs):
    mine, theirs, refs = refs[:4], refs[4:8], refs[8:]
    bits_ref, bias_ref, norm_ref, x_ref, dy_ref, x_far_ref, dy_far_ref = refs[:7]
    refs = refs[7:]
    before, after = refs[:4], refs[4:8]
    db_ref, keep_ref, send_ref, wa_ref, n_ref, nt_ref, n_far_ref, nt_far_ref = refs[8:16]
    out_ref, dn_ref, out_far_ref, dn_far_ref, g1_ref, g2_ref, w1_ref, w2_ref = refs[16:]
    second_norm(x_ref, norm_ref, n_ref, nt_ref)
    second_norm(x_far_ref, norm_ref, n_far_ref, nt_far_ref)

    def put(row, ref):
        for i, w in enumerate((w1_ref, w2_ref, wa_ref)):
            w[pl.ds(row, 96), :] = ref[pl.ds(96 * i, 96), :]

    place_strips(bits_ref, mine, theirs, put)
    for i in range(3):
        cols = slice(256 * i, 256 * (i + 1))
        one = mlp_block(i, n_ref, nt_ref, dy_ref, w1_ref, w2_ref, bias_ref)
        add(i, out_ref, one[0])
        add(i, dn_ref, one[1])
        two = mlp_block(i, n_far_ref, nt_far_ref, dy_far_ref, w1_ref, w2_ref, bias_ref)
        add(i, out_far_ref, two[0])
        add(i, dn_far_ref, two[1])
        g1_ref[:, cols] = one[2] + two[2]
        g2_ref[cols, :] = one[3] + two[3]
        db_ref[:, cols] = one[4] + two[4]
    for old, new, total in zip(before, after, (out_ref, dn_ref, out_far_ref, dn_far_ref)):
        new[...] = (total[...] + old[...].astype(F32)).astype(BF)
    split_gradients(bits_ref, (g1_ref, g2_ref), keep_ref, send_ref)


def mlp_other(*args):
    outs = [((HALF, 768), BF, False)] * 4
    outs += [((8, 768), F32, False)] + SPLIT_OUTS + [((768, 768), BF, False)]
    scratch = NORMED * 2 + SUMS * 2 + [((768, 768), F32)] * 2 + [((768, 768), BF)] * 2
    return call(mlp_other_kernel, "mlp_other", args, outs, scratch, 72 * 10**8, 2 * 10**6, 40)


def finish_kernel(kinds, bits_ref, *refs):
    mine, theirs, outs = refs[:4], refs[4:8], refs[8:]
    full = outs if kinds == 2 else outs[2:]

    def put(row, ref):
        for i, out in enumerate(full):
            out[pl.ds(row, 96), :] = ref[pl.ds(96 * i, 96), :].astype(F32)

    place_strips(bits_ref, mine, theirs, put)
    if kinds == 1:
        outs[0][...] = full[0][pl.ds(0, 576), :]
        outs[1][...] = full[0][pl.ds(576, 192), :]


def finish(kinds, bits, mine, theirs):
    shapes = [(768, 768), (768, 768)] if kinds == 2 else [(576, 768), (192, 768)]
    kernel = lambda *refs: finish_kernel(kinds, *refs)
    scratch = [] if kinds == 2 else [((768, 768), F32)]
    return call(kernel, "finish", (bits, *mine, *theirs), [(s, F32, False) for s in shapes], scratch)


def attn_backward_kernel(last, *refs):
    bits_ref, qkv_ref, kt_ref, lse_ref, ot_ref, n_ref, dy_own_ref, dy_far_ref, w_ref, cos_ref, sin_ref, db_ref = refs[:12]
    if last:
        in_ref, dn2_ref, dn2_far_ref, x_ref, x_far_ref, norm_ref = refs[12:18]
        keep_ref, send_ref, e_keep_ref, e_send_ref = refs[18:22]
        dn_ref = refs[-8]
    else:
        keep_ref, send_ref, dn_ref = refs[12:15]
    dy_ref, do_ref, dk_ref, dv_ref, dt_ref, d_ref, g_ref = refs[-7:]
    own, far = own_rows(bits_ref)
    dy_ref[own, :] = dy_own_ref[...]
    dy_ref[far, :] = dy_far_ref[...]
    dy = dy_ref[...]
    do_ref[0] = nt(dy, w_ref[pl.ds(576, 128), :]).astype(BF)
    do_ref[1] = nt(dy, w_ref[pl.ds(640, 128), :]).astype(BF)
    dk_ref[...] = jnp.zeros_like(dk_ref)
    dv_ref[...] = jnp.zeros_like(dv_ref)
    for h, (qt, qh, kt, vt, vh) in enumerate(HEADS):
        a = h // 2
        rows = pl.ds(64 * h, 64)
        for j in range(NB):
            cols = pl.ds(j * BQ, BQ)
            past = pl.ds(0, j * BQ)
            q = masked(qkv_ref[cols, tile(qt)], qh)
            do = masked(do_ref[a, cols, :], vh)
            lse = lse_ref[pl.ds(h, 1), cols]
            p_d = jnp.exp(causal(nt(qkv_ref[cols, tile(kt)], q), -1e30) - lse)
            dp_d = nt(qkv_ref[cols, tile(vt)], do)
            delta = jnp.sum(p_d * dp_d, axis=0, keepdims=True)
            if j:
                p = jnp.exp(nt(qkv_ref[past, tile(kt)], q) - lse)
                dp = nt(qkv_ref[past, tile(vt)], do)
                delta = delta + jnp.sum(p * dp, axis=0, keepdims=True)
            ds_d = (p_d * (dp_d - delta)).astype(BF)
            dv_ref[a, cols, :] += nn(p_d.astype(BF), do)
            dk_ref[a, cols, :] += nn(ds_d, q)
            dqt = nn(kt_ref[rows, cols], ds_d)
            if j:
                ds = (p * (dp - delta)).astype(BF)
                dv_ref[a, past, :] += nn(p.astype(BF), do)
                dk_ref[a, past, :] += nn(ds, q)
                dqt = dqt + nn(kt_ref[rows, past], ds)
            dt_ref[rows, cols] = dqt * 0.125
    dt_ref[pl.ds(192, 128), :] = dk_ref[0].T
    dt_ref[pl.ds(320, 64), :] = dk_ref[1].T[:64]
    dt_ref[pl.ds(384, 128), :] = dv_ref[0].T
    dt_ref[pl.ds(512, 64), :] = dv_ref[1].T[64:]
    dt_ref[pl.ds(576, 64), :] = jnp.zeros((64, SEQ), F32)
    cos, sin = cos_ref[...], sin_ref[...]
    for at in ROTATED:
        one, two = dt_ref[pl.ds(at, 8), :], dt_ref[pl.ds(at + 8, 8), :]
        dt_ref[pl.ds(at, 8), :] = one * cos + two * sin
        dt_ref[pl.ds(at + 8, 8), :] = two * cos - one * sin
    for i in range(5):
        d_ref[:, tile(i)] = dt_ref[tile(i), :].T.astype(BF)
    d = d_ref[...]
    g_ref[pl.ds(0, 576), :] = nn(dt_ref[pl.ds(0, 576), :].astype(BF), n_ref[...])
    g_ref[pl.ds(576, 192), :] = nn(ot_ref[...], dy)
    dn = nn(d, w_ref[pl.ds(0, 640), :])

    core = bits_ref[0]
    keep_ref[...] = g_ref[pl.ds(pl.multiple_of(384 * core, 384), 384), :].astype(BF)
    send_ref[pl.ds(0, 384), :] = g_ref[pl.ds(pl.multiple_of(384 - 384 * core, 384), 384), :].astype(BF)
    row = lax.broadcasted_iota(jnp.int32, (8, 768), 0)
    columns = jnp.concatenate([nn(jnp.ones((8, SEQ), BF), d), jnp.zeros((8, 128), F32)], 1)
    vec = jnp.where(row == 0, db_ref[...], jnp.where(row == 1, columns, 0.0))
    if last:
        dn_ref[...] = dn + in_ref[...]
        gain1, gain2 = norm_ref[0:1], norm_ref[2:3]
        sums = [0.0] * 4
        for rows, dn2_rows, x_rows in ((own, dn2_ref, x_ref), (far, dn2_far_ref, x_far_ref)):
            dn1, dn2, x = dn_ref[rows, :], dn2_rows[...].astype(F32), x_rows[...].astype(F32)
            e = dn1 * gain1 + dn2 * gain2
            if rows is own:
                e_keep_ref[...] = e
            else:
                e_send_ref[...] = e.astype(BF)
            centered = x - jnp.mean(x, axis=-1, keepdims=True)
            xhat = centered * lax.rsqrt(jnp.mean(centered * centered, axis=-1, keepdims=True) + EPS)
            for i, term in enumerate((dn1 * xhat, dn1, dn2 * xhat, dn2)):
                sums[i] = sums[i] + jnp.sum(term, axis=0, keepdims=True)
        sums.append(jnp.sum(dy_own_ref[...].astype(F32), axis=0, keepdims=True))
        for i, value in enumerate(sums):
            vec = jnp.where(row == 2 + i, value, vec)
    else:
        dn_ref[...] = dn
    high = vec.astype(BF)
    send_ref[pl.ds(384, 16), :] = jnp.concatenate([high, (vec - high.astype(F32)).astype(BF)], 0)


def attn_backward(last, *args):
    outs = [((384, 768), BF, False), ((400, 768), BF, False)]
    if last:
        outs += [((HALF, 768), F32, False), ((HALF, 768), BF, False)]
    else:
        outs += [((SEQ, 768), F32, True)]
    scratch = [
        ((SEQ, 768), BF),
        ((2, SEQ, 128), BF),
        ((2, SEQ, 128), F32),
        ((2, SEQ, 128), F32),
        ((640, SEQ), F32),
        ((SEQ, 640), BF),
        ((768, 768), F32),
    ]
    if last:
        scratch.insert(0, ((SEQ, 768), F32))
    kernel = lambda *refs: attn_backward_kernel(last, *refs)
    return call(kernel, "attn_backward", args, outs, scratch, 5 * 10**9, 10**6, 40)


def swap(value, axis, distance):
    size = lax.axis_size(axis)
    return lax.ppermute(value, axis, [(i, i ^ distance) for i in range(size)])


def bit_of(axis, distance):
    return (lax.axis_index(axis) // distance) % 2


def exact(vec):
    high = lax.reduce_precision(vec, 8, 7)
    return jnp.concatenate([high.astype(BF), (vec - high).astype(BF)], 0)


def joined(pair):
    rows = pair.shape[0] // 2
    return pair[:rows].astype(F32) + pair[rows:].astype(F32)


def spot():
    return 2 * bit_of("dp", 2) + bit_of("dp", 4)


PEERS = ((4, 1), (2, 2), (6, 3))


def messages(keep, got, vec=None):
    def part(change):
        at = (spot() ^ change) * 96
        cut = lambda v: lax.dynamic_slice_in_dim(v, at, 96, 1).astype(F32)
        return cut(keep) + cut(got)

    out = []
    for _, change in PEERS:
        sent = part(change).astype(BF).reshape(-1, keep.shape[-1])
        out.append(sent if vec is None else jnp.concatenate([sent, exact(vec)], 0))
    return part(0), out


def exchange(out):
    return [swap(message, "dp", distance) for (distance, _), message in zip(PEERS, out)]


def summed(own, got, vec=None):
    rows = own.shape[0] * 96
    total = own
    for message in got:
        total = total + message[:rows].reshape(own.shape).astype(F32)
    if vec is None:
        return total
    y, x, both = (joined(message[rows:]) for message in got)
    return total, (joined(exact(vec)) + y) + (x + both)


def core_swap(parts):
    return [swap(part, "dp", 1) for part in parts]


def far_sum(value):
    distance = 8
    while distance < lax.axis_size("dp"):
        mine = lax.reduce_precision(value, 8, 7)
        value = mine + swap(mine.astype(BF), "dp", distance).astype(F32)
        distance *= 2
    return value


def far_sum_exact(vec):
    distance = 8
    while distance < lax.axis_size("dp"):
        mine = exact(vec)
        vec = joined(mine) + joined(swap(mine, "dp", distance))
        distance *= 2
    return vec


def rotary_tables(rot_dims):
    position = jnp.arange(SEQ).astype(F32)
    inverse = 1.0 / 10000.0 ** (jnp.arange(0, rot_dims, 2).astype(F32) / rot_dims)
    angles = inverse[:, None] * position[None, :]
    return jnp.cos(angles), jnp.sin(angles)


def tied(values, *others):
    return lax.optimization_barrier((values, others))[0]


def body(
    tokens, cotangent, attention_norm_gain, attention_norm_bias, feedforward_norm_gain, feedforward_norm_bias,
    w_qkv, bias_qv, bias_key, w_dense, bias_dense, w_fc1, bias_fc1, w_fc2, bias_fc2,
):
    width = tokens.shape[1]
    rot_dims = bias_key.shape[1]
    core = bit_of("dp", 1)
    bits = jnp.stack([core, bit_of("tensor", 1), spot()]).astype(jnp.int32)

    x_far = swap(tokens, "tensor", 1)

    wa = jnp.concatenate([w_qkv.transpose(1, 2, 0).reshape(-1, width), w_dense], 0)
    key_bias = jnp.pad(bias_key, ((0, 0), (0, 64 - rot_dims))).reshape(192)
    bias = jnp.stack([jnp.concatenate([bias_qv[0], key_bias, bias_qv[1], jnp.zeros((192,), F32)]), bias_fc1])
    at = (4 * core + spot()) * 96
    pieces = jnp.concatenate([lax.dynamic_slice_in_dim(w, at, 96, 0) for w in (w_fc1, w_fc2, wa)], 0)
    pieces_far = swap(pieces, "tensor", 2)
    bias_far = swap(bias, "tensor", 2)
    rotary = rotary_tables(rot_dims)
    pad8 = lambda row: jnp.broadcast_to(row[None], (8, width))
    norms = jnp.stack([attention_norm_gain, attention_norm_bias, feedforward_norm_gain, feedforward_norm_bias])

    b1 = pad8(bias[1])
    mlp_out, dn2, db, g1, g2 = mlp_half(True, tokens, norms, cotangent, w_fc1, w_fc2, b1)
    x_far = tied(x_far, g1)
    dy_far = swap(tied(cotangent, x_far), "tensor", 1)

    x_far, pieces_far, bias_far = tied((x_far, pieces_far, bias_far), pieces_far, bias_far)
    got = exchange([pieces_far] * 3)
    n1, *saved, ot = attn_forward(True, bits, tokens, x_far, norms, wa, pad8(bias[0]), *rotary)
    dy_far, ot = tied((dy_far, ot), dy_far)
    mlp_out_far, dn2_far, db, keep, send = mlp_half(
        False, tied(x_far, ot), norms, dy_far, w_fc1, w_fc2, b1, bits, db, *near((g1, g2))
    )
    keep, send, got = tied((keep, send, got), got)
    send_far = swap(send, "dp", 1)
    mine = [pieces_far, *got]
    theirs = core_swap(mine)
    fc_own, sent = messages(keep, send_far)
    fc_got = exchange(sent)

    mlp_out, dn2, mlp_out_far, dn2_far, db_far, keep, send, wa_far = mlp_other(
        *mine, *theirs, bits, pad8(bias_far[1]), norms, tokens, cotangent, x_far, dy_far,
        *away((mlp_out, tied(dn2, sent), mlp_out_far, dn2_far)),
    )
    keep, send, wa_far, fc_got = tied((keep, send, wa_far, fc_got), fc_got)
    send_far = swap(send, "dp", 1)
    fc_own = summed(fc_own, fc_got)
    fc_far, sent = messages(keep, send_far)
    got = exchange(sent)
    n1, wa_far, ot = away((n1, tied(wa_far, fc_own, sent), ot))
    *saved_far, out_keep, out_send = attn_forward(
        False, bits, n1, wa_far, pad8(bias_far[0]), *rotary, ot, w_dense, *away((mlp_out, mlp_out_far)),
    )
    out_send, saved_far, got = tied((out_send, saved_far, got), got)
    fc_far = summed(fc_far, got).astype(BF)
    fc_far_in = swap(fc_far, "tensor", 2)
    out_far = swap(tied(out_send, fc_far), "tensor", 1)
    qkv, kt, lse, ot_far = tied(saved_far, fc_far)
    keep, send, dn1 = attn_backward(
        False, bits, near(qkv), near(kt), lse, near(ot_far), n1, cotangent, dy_far, wa_far, *rotary, db_far
    )
    keep, send, dn1, fc_far_in = tied((keep, send, dn1, fc_far_in), fc_far_in)
    send_far = swap(send, "dp", 1)
    vec_far = joined(send[384:]) + joined(send_far[384:])
    a_far, sent = messages(keep[None], send_far[None, :384], vec_far)
    fc_grad = lax.reduce_precision(far_sum(fc_own + fc_far_in.astype(F32)), 8, 7).astype(BF).reshape(192, width)
    sent = [jnp.concatenate([message, fc_grad], 0) for message in sent]
    got = exchange(sent)
    keep, send, e_keep, e_send = attn_backward(
        True, bits, *away((*saved, ot)), n1, cotangent, dy_far, wa, *rotary, db, near(tied(dn1, sent)),
        *away((dn2, dn2_far)), tokens, x_far, norms,
    )
    keep, send, e_keep, e_send, got, out_far = tied((keep, send, e_keep, e_send, got, out_far), got, out_far)

    send_far = swap(send, "dp", 1)
    a_far, vec_far = summed(a_far, [message[:112] for message in got], vec_far)
    far_send = jnp.concatenate([a_far[0].astype(BF), exact(vec_far)], 0)
    far = swap(far_send, "tensor", 2)
    e_far = swap(tied(e_send, far_send), "tensor", 1)
    vec = joined(send[384:]) + joined(send_far[384:])
    a_own, sent = messages(keep[None], send_far[None, :384], vec)
    a_got = exchange(sent)
    fc_mine = jnp.stack([fc_grad, *(message[112:] for message in tied(got, sent))])
    own_tokens = tokens.astype(F32)
    mixed_out = (own_tokens + (out_keep + tied(out_far, sent).astype(F32)) + bias_dense + bias_fc2).astype(BF)
    a_own, vec = summed(a_own, tied(a_got, fc_mine, mixed_out), vec)
    a_grad = lax.reduce_precision(far_sum(a_own + far[None, :96].astype(F32)), 8, 7).astype(BF).reshape(96, width)
    a_got = exchange([a_grad] * 3)
    fc_mine = tied(fc_mine, a_grad)
    fc1_grad, fc2_grad = finish(2, bits, list(fc_mine), list(swap(fc_mine, "dp", 1)))
    e_far = tied(e_far, a_grad)
    quarter_vec = far_sum_exact(vec + joined(far[96:]))
    vec = tied(far_sum_exact(vec), a_grad)
    for distance in (1, 2):
        packet = exact(vec)
        vec = joined(packet) + joined(swap(packet, "tensor", distance))

    e = e_keep + e_far.astype(F32)
    centered = own_tokens - jnp.mean(own_tokens, axis=-1, keepdims=True)
    r = lax.rsqrt(jnp.mean(centered * centered, axis=-1, keepdims=True) + EPS)
    xhat = centered * r
    dx = r * (e - jnp.mean(e, axis=-1, keepdims=True) - xhat * jnp.mean(e * xhat, axis=-1, keepdims=True))
    grad_tokens = (cotangent.astype(F32) + dx).astype(BF)

    mine = tied([a_grad, *a_got], fc1_grad)
    qkv_grad, dense_grad = finish(1, bits, mine, core_swap(mine))
    columns = quarter_vec[1]
    return (
        mixed_out,
        grad_tokens,
        vec[2],
        vec[3],
        vec[4],
        vec[5],
        qkv_grad.reshape(3, 192, width).transpose(2, 0, 1),
        jnp.stack([columns[:192], columns[384:576]]),
        columns[192:384].reshape(3, 64)[:, :rot_dims],
        dense_grad,
        vec[6],
        fc1_grad,
        quarter_vec[0],
        fc2_grad,
        vec[6],
    )


def solution(mesh):
    rows = P(("dp", "tensor"), None)
    in_specs = (
        rows, rows, P(), P(), P(), P(), P(None, None, "tensor"), P(None, "tensor"), P("tensor", None),
        P("tensor", None), P(), P(None, "tensor"), P("tensor"), P("tensor", None), P(),
    )
    out_specs = (
        rows, rows, P(), P(), P(), P(), P(None, None, "tensor"), P(None, "tensor"), P("tensor", None),
        P("tensor", None), P(), P(None, "tensor"), P("tensor"), P("tensor", None), P(),
    )
    return jax.shard_map(body, mesh=mesh, in_specs=in_specs, out_specs=out_specs, check_vma=False)
```

```python
import math

import jax
import jax.numpy as jnp
from jax import lax
from jax.experimental import pallas as pl
from jax.experimental.pallas import tpu as pltpu
from jax.sharding import PartitionSpec as P

SEQ = 1024
EPS = 1e-05
BF = jnp.bfloat16
F32 = jnp.float32
BQ = 256
NB = SEQ // BQ
HALF = SEQ // 2


def nn(a, b):
    return lax.dot_general(a, b, (((1,), (0,)), ((), ())), preferred_element_type=F32)


def nt(a, b):
    return lax.dot_general(a, b, (((1,), (1,)), ((), ())), preferred_element_type=F32)


def call(kernel, name, args, outs, scratch=(), flops=0, transcendentals=0, limit=28):
    moved = sum(a.size * a.dtype.itemsize for a in args) + sum(math.prod(o[0]) * jnp.dtype(o[1]).itemsize for o in outs)
    spaces = [pltpu.SMEM if a.dtype == jnp.int32 else pltpu.VMEM for a in args]
    return pl.pallas_call(
        kernel,
        in_specs=[pl.BlockSpec(memory_space=s) for s in spaces],
        out_specs=[pl.BlockSpec(memory_space=pltpu.VMEM)] * len(outs),
        out_shape=[(pltpu.VMEM if stays else pltpu.HBM)(s, d) for s, d, stays in outs],
        scratch_shapes=[pltpu.VMEM(s, d) for s, d in scratch],
        compiler_params=pltpu.CompilerParams(vmem_limit_bytes=limit * 2**20),
        cost_estimate=pl.CostEstimate(flops=flops, bytes_accessed=moved, transcendentals=transcendentals),
        name=name,
    )(*args)


def near(values):
    return jax.tree.map(lambda v: pltpu.with_memory_space_constraint(v, pltpu.VMEM), values)


def away(values):
    return jax.tree.map(lambda v: pltpu.with_memory_space_constraint(v, pltpu.HBM), values)


def own_rows(bits_ref):
    half = bits_ref[1]
    return pl.ds(pl.multiple_of(HALF * half, HALF), HALF), pl.ds(pl.multiple_of(HALF - HALF * half, HALF), HALF)


def place_strips(bits_ref, mine, theirs, put):
    for slot in range(4):
        at = 96 * (bits_ref[2] ^ slot)
        put(pl.multiple_of(384 * bits_ref[0] + at, 96), mine[slot])
        put(pl.multiple_of(384 - 384 * bits_ref[0] + at, 96), theirs[slot])


def normalized(x_ref, gain, shift, put):
    for i in range(HALF // BQ):
        rows = pl.ds(i * BQ, BQ)
        x = x_ref[rows, :].astype(F32)
        centered = x - jnp.mean(x, axis=-1, keepdims=True)
        r = lax.rsqrt(jnp.mean(centered * centered, axis=-1, keepdims=True) + EPS)
        put(i * BQ, centered * r * gain + shift)


def tile(i):
    return slice(128 * i, 128 * (i + 1))


HEADS = ((0, 0, 1, 2, 0), (0, 1, 1, 2, 1), (4, 0, 5, 4, 1))
TILES = {0: (0, 64), 1: (192, 256), 2: (384, 448), 4: (128, 512), 5: (320, None)}
ROTATED = (0, 64, 128, 192, 256, 320)


def masked(x, half):
    keep = lax.broadcasted_iota(jnp.int32, x.shape, 1) < 64
    zero = jnp.zeros_like(x)
    return jnp.where(keep, x, zero) if half == 0 else jnp.where(keep, zero, x)


def causal(x, fill):
    rows = lax.broadcasted_iota(jnp.int32, x.shape, 0)
    cols = lax.broadcasted_iota(jnp.int32, x.shape, 1)
    return jnp.where(rows <= cols, x, fill)


def attn_forward_kernel(first, *refs):
    if first:
        bits_ref, x_ref, x_far_ref, norm_ref, w_ref, bias_ref, cos_ref, sin_ref = refs[:8]
        n_ref, qkv_ref, kt_ref, lse_ref, ot_ref, m_ref, o_ref, vt_ref = refs[8:]
        for x, at in ((x_ref, HALF * bits_ref[1]), (x_far_ref, HALF - HALF * bits_ref[1])):
            def put(row, n):
                n_ref[pl.ds(pl.multiple_of(at + row, BQ), BQ), :] = n.astype(BF)

            normalized(x, norm_ref[0:1], norm_ref[1:2], put)
    else:
        bits_ref, n_ref, w_ref, bias_ref, cos_ref, sin_ref, ot_in_ref, wd_in_ref, mlp_ref, mlp_far_ref = refs[:10]
        qkv_ref, kt_ref, lse_ref, ot_ref, keep_ref, send_ref, m_ref, o_ref, vt_ref, out_ref = refs[10:]
    n = n_ref[...]
    bias = bias_ref[...].T
    for at, size in ((0, 256), (256, 320)):
        m_ref[pl.ds(at, size), :] = nt(w_ref[pl.ds(at, size), :], n) + bias[at : at + size, 0:1]
    cos, sin = cos_ref[...], sin_ref[...]
    for at in ROTATED:
        one, two = m_ref[pl.ds(at, 8), :], m_ref[pl.ds(at + 8, 8), :]
        m_ref[pl.ds(at, 8), :] = one * cos - two * sin
        m_ref[pl.ds(at + 8, 8), :] = two * cos + one * sin
    m_ref[pl.ds(0, 192), :] = m_ref[pl.ds(0, 192), :] * 0.125
    for i, (one, two) in TILES.items():
        upper = jnp.zeros((64, SEQ), F32) if two is None else m_ref[pl.ds(two, 64), :]
        qkv_ref[:, tile(i)] = jnp.concatenate([m_ref[pl.ds(one, 64), :], upper], 0).T.astype(BF)
    kt_ref[...] = m_ref[pl.ds(192, 192), :].astype(BF)
    vt_ref[...] = m_ref[pl.ds(384, 192), :].astype(BF)

    lse_ref[...] = jnp.zeros((8, SEQ), F32)
    for h, (qt, qh, kt, vt, vh) in enumerate(HEADS):
        v_rows = pl.ds(64 * h, 64)
        for j in range(NB):
            cols = pl.ds(j * BQ, BQ)
            past = pl.ds(0, j * BQ)
            q = masked(qkv_ref[cols, tile(qt)], qh)
            st_d = causal(nt(qkv_ref[cols, tile(kt)], q), -1e30)
            top = jnp.max(st_d, axis=0, keepdims=True)
            if j:
                st = nt(qkv_ref[past, tile(kt)], q)
                top = jnp.maximum(top, jnp.max(st, axis=0, keepdims=True))
            w_d = jnp.exp(st_d - top)
            total = jnp.sum(w_d, axis=0, keepdims=True)
            o = nn(vt_ref[v_rows, cols], w_d.astype(BF))
            if j:
                w = jnp.exp(st - top)
                total = total + jnp.sum(w, axis=0, keepdims=True)
                o = o + nn(vt_ref[v_rows, past], w.astype(BF))
            o_ref[pl.ds(64 * h, 64), cols] = o * (1.0 / total)
            lse_ref[pl.ds(h, 1), cols] = top + jnp.log(total)
    ot_ref[...] = o_ref[...].astype(BF)
    if not first:
        own, far = own_rows(bits_ref)
        out_ref[...] = nn(o_ref[...].T.astype(BF), w_ref[pl.ds(576, 192), :]) + nn(
            ot_in_ref[...].astype(F32).T.astype(BF), wd_in_ref[...]
        )
        keep_ref[...] = out_ref[own, :] + mlp_ref[...].astype(F32)
        send_ref[...] = (out_ref[far, :] + mlp_far_ref[...].astype(F32)).astype(BF)


def attn_forward(first, *args):
    outs = [
        ((SEQ, 768), BF, False),
        ((SEQ, 768), BF, not first),
        ((192, SEQ), BF, not first),
        ((8, SEQ), F32, False),
        ((192, SEQ), BF, not first),
    ]
    scratch = [((576, SEQ), F32), ((192, SEQ), F32), ((192, SEQ), BF)]
    if not first:
        outs = outs[1:] + [((HALF, 768), F32, False), ((HALF, 768), BF, False)]
        scratch.append(((SEQ, 768), F32))
    kernel = lambda *refs: attn_forward_kernel(first, *refs)
    return call(kernel, "attn_forward", args, outs, scratch, 4 * 10**9, 2 * 10**6)


def normal_cdf(hidden):
    return 0.5 * (1.0 + lax.erf(hidden * math.sqrt(0.5)))


def mlp_hidden(n_ref, dy_ref, w1_ref, w2_ref, bias_ref, a_ref, dh_ref, db_ref):
    dy = dy_ref[...]
    for i in range(3):
        cols = slice(256 * i, 256 * (i + 1))
        hidden = nn(n_ref[...], w1_ref[:, cols]) + bias_ref[0:1, cols]
        cdf = normal_cdf(hidden)
        a_ref[:, cols] = (hidden * cdf).astype(BF)
        slope = cdf + hidden * (jnp.exp(-0.5 * hidden * hidden) * (1.0 / math.sqrt(2.0 * math.pi)))
        dh = (nt(dy, w2_ref[cols, :]) * slope).astype(BF)
        dh_ref[:, cols] = dh
        db_ref[:, cols] = jnp.broadcast_to(jnp.sum(dh.astype(F32), axis=0, keepdims=True), (8, 256))


def split_gradients(bits_ref, grads, keep_ref, send_ref):
    core = bits_ref[0]
    for i, g in enumerate(grads):
        keep_ref[i] = g[pl.ds(pl.multiple_of(384 * core, 384), 384), :].astype(BF)
        send_ref[i] = g[pl.ds(pl.multiple_of(384 - 384 * core, 384), 384), :].astype(BF)


def second_norm(x_ref, norm_ref, n_ref, nt_ref, at=0):
    def put(row, n):
        n_ref[pl.ds(at + row, BQ), :] = n.astype(BF)
        nt_ref[:, pl.ds(at + row, BQ)] = n.T.astype(BF)

    normalized(x_ref, norm_ref[2:3], norm_ref[3:4], put)


def mlp_half_kernel(first, *refs):
    if first:
        x_ref, norm_ref, dy_ref, w1_ref, w2_ref, bias_ref = refs[:6]
        out_ref, dn_ref, db_ref, g1_ref, g2_ref, n_ref, nt_ref, a_ref, dh_ref = refs[6:]
    else:
        x_ref, norm_ref, dy_ref, w1_ref, w2_ref, bias_ref, bits_ref, db_in_ref, g1_in_ref, g2_in_ref = refs[:10]
        out_ref, dn_ref, db_ref, keep_ref, send_ref, n_ref, nt_ref, a_ref, dh_ref, g1_ref, g2_ref = refs[10:]
    second_norm(x_ref, norm_ref, n_ref, nt_ref)
    mlp_hidden(n_ref, dy_ref, w1_ref, w2_ref, bias_ref, a_ref, dh_ref, db_ref)
    g1, g2 = nn(nt_ref[...], dh_ref[...]), nn(a_ref[...].T, dy_ref[...])
    g1_ref[...] = g1 if first else g1 + g1_in_ref[...]
    g2_ref[...] = g2 if first else g2 + g2_in_ref[...]
    out_ref[...] = nn(a_ref[...], w2_ref[...]).astype(BF)
    dn_ref[...] = nt(dh_ref[...], w1_ref[...]).astype(BF)
    if not first:
        db_ref[...] += db_in_ref[...]
        split_gradients(bits_ref, (g1_ref, g2_ref), keep_ref, send_ref)


SPLIT_OUTS = [((2, 384, 768), BF, False)] * 2


def mlp_half(first, *args):
    grads = [((768, 768), F32, True)] * 2
    outs = [((HALF, 768), BF, False)] * 2 + [((8, 768), F32, False)] + (grads if first else SPLIT_OUTS)
    scratch = [((HALF, 768), BF), ((768, HALF), BF), ((HALF, 768), BF), ((HALF, 768), BF)] + ([] if first else [g[:2] for g in grads])
    kernel = lambda *refs: mlp_half_kernel(first, *refs)
    return call(kernel, "mlp_half", args, outs, scratch, 36 * 10**8, 10**6)


def mlp_other_kernel(*refs):
    mine, theirs, refs = refs[:4], refs[4:8], refs[8:]
    bits_ref, bias_ref, norm_ref, x_ref, dy_ref, x_far_ref, dy_far_ref = refs[:7]
    refs = refs[7:]
    before, after = refs[:4], refs[4:8]
    db_ref, keep_ref, send_ref, wa_ref, n_ref, nt_ref, dy_all_ref, a_ref, dh_ref = refs[8:17]
    g1_ref, g2_ref, w1_ref, w2_ref = refs[17:]
    second_norm(x_ref, norm_ref, n_ref, nt_ref)
    second_norm(x_far_ref, norm_ref, n_ref, nt_ref, HALF)
    dy_all_ref[pl.ds(0, HALF), :] = dy_ref[...]
    dy_all_ref[pl.ds(HALF, HALF), :] = dy_far_ref[...]

    def put(row, ref):
        for i, w in enumerate((w1_ref, w2_ref, wa_ref)):
            w[pl.ds(row, 96), :] = ref[pl.ds(96 * i, 96), :]

    place_strips(bits_ref, mine, theirs, put)
    mlp_hidden(n_ref, dy_all_ref, w1_ref, w2_ref, bias_ref, a_ref, dh_ref, db_ref)
    g1_ref[...] = nn(nt_ref[...], dh_ref[...])
    g2_ref[...] = nn(a_ref[...].T, dy_all_ref[...])
    for half in range(2):
        rows = pl.ds(HALF * half, HALF)
        old, new = before[2 * half : 2 * half + 2], after[2 * half : 2 * half + 2]
        new[0][...] = (nn(a_ref[rows, :], w2_ref[...]) + old[0][...].astype(F32)).astype(BF)
        new[1][...] = (nt(dh_ref[rows, :], w1_ref[...]) + old[1][...].astype(F32)).astype(BF)
    split_gradients(bits_ref, (g1_ref, g2_ref), keep_ref, send_ref)


def mlp_other(*args):
    outs = [((HALF, 768), BF, False)] * 4
    outs += [((8, 768), F32, False)] + SPLIT_OUTS + [((768, 768), BF, False)]
    scratch = [((SEQ, 768), BF), ((768, SEQ), BF)] + [((SEQ, 768), BF)] * 3 + [((768, 768), F32)] * 2 + [((768, 768), BF)] * 2
    return call(mlp_other_kernel, "mlp_other", args, outs, scratch, 72 * 10**8, 2 * 10**6, 40)


def finish_kernel(kinds, bits_ref, *refs):
    mine, theirs = ([ref.at[slot] for slot in range(4)] for ref in refs[:2])
    outs = refs[2:]
    full = outs if kinds == 2 else outs[2:]

    def put(row, ref):
        for i, out in enumerate(full):
            out[pl.ds(row, 96), :] = ref[pl.ds(96 * i, 96), :].astype(F32)

    place_strips(bits_ref, mine, theirs, put)
    if kinds == 1:
        outs[0][...] = full[0][pl.ds(0, 576), :]
        outs[1][...] = full[0][pl.ds(576, 192), :]


def finish(kinds, bits, mine, theirs):
    shapes = [(768, 768), (768, 768)] if kinds == 2 else [(576, 768), (192, 768)]
    kernel = lambda *refs: finish_kernel(kinds, *refs)
    scratch = [] if kinds == 2 else [((768, 768), F32)]
    return call(kernel, "finish", (bits, mine, theirs), [(s, F32, False) for s in shapes], scratch)


def attn_backward_kernel(last, *refs):
    bits_ref, qkv_ref, kt_ref, lse_ref, ot_ref, n_ref, dy_own_ref, dy_far_ref, w_ref, cos_ref, sin_ref, db_ref = refs[:12]
    if last:
        in_ref, dn2_ref, dn2_far_ref, x_ref, x_far_ref, norm_ref = refs[12:18]
        keep_ref, send_ref, e_keep_ref, e_send_ref = refs[18:22]
        dn_ref = refs[-8]
    else:
        keep_ref, send_ref, dn_ref = refs[12:15]
    dy_ref, do_ref, dk_ref, dv_ref, dt_ref, d_ref, g_ref = refs[-7:]
    own, far = own_rows(bits_ref)
    dy_ref[own, :] = dy_own_ref[...]
    dy_ref[far, :] = dy_far_ref[...]
    dy = dy_ref[...]
    do_ref[0] = nt(dy, w_ref[pl.ds(576, 128), :]).astype(BF)
    do_ref[1] = nt(dy, w_ref[pl.ds(640, 128), :]).astype(BF)
    dk_ref[...] = jnp.zeros_like(dk_ref)
    dv_ref[...] = jnp.zeros_like(dv_ref)
    for h, (qt, qh, kt, vt, vh) in enumerate(HEADS):
        a = h // 2
        rows = pl.ds(64 * h, 64)
        for j in range(NB):
            cols = pl.ds(j * BQ, BQ)
            past = pl.ds(0, j * BQ)
            q = masked(qkv_ref[cols, tile(qt)], qh)
            do = masked(do_ref[a, cols, :], vh)
            lse = lse_ref[pl.ds(h, 1), cols]
            p_d = jnp.exp(causal(nt(qkv_ref[cols, tile(kt)], q), -1e30) - lse)
            dp_d = nt(qkv_ref[cols, tile(vt)], do)
            delta = jnp.sum(p_d * dp_d, axis=0, keepdims=True)
            if j:
                p = jnp.exp(nt(qkv_ref[past, tile(kt)], q) - lse)
                dp = nt(qkv_ref[past, tile(vt)], do)
                delta = delta + jnp.sum(p * dp, axis=0, keepdims=True)
            ds_d = (p_d * (dp_d - delta)).astype(BF)
            dv_ref[a, cols, :] += nn(p_d.astype(BF), do)
            dk_ref[a, cols, :] += nn(ds_d, q)
            dqt = nn(kt_ref[rows, cols], ds_d)
            if j:
                ds = (p * (dp - delta)).astype(BF)
                dv_ref[a, past, :] += nn(p.astype(BF), do)
                dk_ref[a, past, :] += nn(ds, q)
                dqt = dqt + nn(kt_ref[rows, past], ds)
            dt_ref[rows, cols] = dqt * 0.125
    dt_ref[pl.ds(192, 128), :] = dk_ref[0].T
    dt_ref[pl.ds(320, 64), :] = dk_ref[1].T[:64]
    dt_ref[pl.ds(384, 128), :] = dv_ref[0].T
    dt_ref[pl.ds(512, 64), :] = dv_ref[1].T[64:]
    dt_ref[pl.ds(576, 64), :] = jnp.zeros((64, SEQ), F32)
    cos, sin = cos_ref[...], sin_ref[...]
    for at in ROTATED:
        one, two = dt_ref[pl.ds(at, 8), :], dt_ref[pl.ds(at + 8, 8), :]
        dt_ref[pl.ds(at, 8), :] = one * cos + two * sin
        dt_ref[pl.ds(at + 8, 8), :] = two * cos - one * sin
    for i in range(5):
        d_ref[:, tile(i)] = dt_ref[tile(i), :].T.astype(BF)
    d = d_ref[...]
    g_ref[pl.ds(0, 576), :] = nn(dt_ref[pl.ds(0, 576), :].astype(BF), n_ref[...])
    g_ref[pl.ds(576, 192), :] = nn(ot_ref[...], dy)
    dn = nn(d, w_ref[pl.ds(0, 640), :])

    core = bits_ref[0]
    keep_ref[...] = g_ref[pl.ds(pl.multiple_of(384 * core, 384), 384), :].astype(BF)
    send_ref[pl.ds(0, 384), :] = g_ref[pl.ds(pl.multiple_of(384 - 384 * core, 384), 384), :].astype(BF)
    row = lax.broadcasted_iota(jnp.int32, (8, 768), 0)
    columns = jnp.concatenate([nn(jnp.ones((8, SEQ), BF), d), jnp.zeros((8, 128), F32)], 1)
    vec = jnp.where(row == 0, db_ref[...], jnp.where(row == 1, columns, 0.0))
    if last:
        dn_ref[...] = dn + in_ref[...]
        gain1, gain2 = norm_ref[0:1], norm_ref[2:3]
        sums = [0.0] * 4
        for rows, dn2_rows, x_rows in ((own, dn2_ref, x_ref), (far, dn2_far_ref, x_far_ref)):
            dn1, dn2, x = dn_ref[rows, :], dn2_rows[...].astype(F32), x_rows[...].astype(F32)
            e = dn1 * gain1 + dn2 * gain2
            if rows is own:
                e_keep_ref[...] = e
            else:
                e_send_ref[...] = e.astype(BF)
            centered = x - jnp.mean(x, axis=-1, keepdims=True)
            xhat = centered * lax.rsqrt(jnp.mean(centered * centered, axis=-1, keepdims=True) + EPS)
            for i, term in enumerate((dn1 * xhat, dn1, dn2 * xhat, dn2)):
                sums[i] = sums[i] + jnp.sum(term, axis=0, keepdims=True)
        sums.append(jnp.sum(dy_own_ref[...].astype(F32), axis=0, keepdims=True))
        for i, value in enumerate(sums):
            vec = jnp.where(row == 2 + i, value, vec)
    else:
        dn_ref[...] = dn
    high = vec.astype(BF)
    send_ref[pl.ds(384, 16), :] = jnp.concatenate([high, (vec - high.astype(F32)).astype(BF)], 0)


def attn_backward(last, *args):
    outs = [((384, 768), BF, False), ((400, 768), BF, False)]
    if last:
        outs += [((HALF, 768), F32, False), ((HALF, 768), BF, False)]
    else:
        outs += [((SEQ, 768), F32, True)]
    scratch = [
        ((SEQ, 768), BF),
        ((2, SEQ, 128), BF),
        ((2, SEQ, 128), F32),
        ((2, SEQ, 128), F32),
        ((640, SEQ), F32),
        ((SEQ, 640), BF),
        ((768, 768), F32),
    ]
    if last:
        scratch.insert(0, ((SEQ, 768), F32))
    kernel = lambda *refs: attn_backward_kernel(last, *refs)
    return call(kernel, "attn_backward", args, outs, scratch, 5 * 10**9, 10**6, 40)


def swap(value, axis, distance):
    size = lax.axis_size(axis)
    return lax.ppermute(value, axis, [(i, i ^ distance) for i in range(size)])


def bit_of(axis, distance):
    return (lax.axis_index(axis) // distance) % 2


def exact(vec):
    high = lax.reduce_precision(vec, 8, 7)
    return jnp.concatenate([high.astype(BF), (vec - high).astype(BF)], 0)


def joined(pair):
    rows = pair.shape[0] // 2
    return pair[:rows].astype(F32) + pair[rows:].astype(F32)


def spot():
    return 2 * bit_of("dp", 2) + bit_of("dp", 4)


PEERS = ((4, 1), (2, 2), (6, 3))


def messages(keep, got, vec=None):
    def part(change):
        at = (spot() ^ change) * 96
        cut = lambda v: lax.dynamic_slice_in_dim(v, at, 96, 1).astype(F32)
        return cut(keep) + cut(got)

    out = []
    for _, change in PEERS:
        sent = part(change).astype(BF).reshape(-1, keep.shape[-1])
        out.append(sent if vec is None else jnp.concatenate([sent, exact(vec)], 0))
    return part(0), out


def exchange(out):
    return [swap(message, "dp", distance) for (distance, _), message in zip(PEERS, out)]


def summed(own, got, vec=None):
    rows = own.shape[0] * 96
    total = own
    for message in got:
        total = total + message[:rows].reshape(own.shape).astype(F32)
    if vec is None:
        return total
    y, x, both = (joined(message[rows:]) for message in got)
    return total, (joined(exact(vec)) + y) + (x + both)


def core_swap(parts):
    return [swap(part, "dp", 1) for part in parts]


def far_sum(value):
    distance = 8
    while distance < lax.axis_size("dp"):
        mine = lax.reduce_precision(value, 8, 7)
        value = mine + swap(mine.astype(BF), "dp", distance).astype(F32)
        distance *= 2
    return value


def far_sum_exact(vec):
    distance = 8
    while distance < lax.axis_size("dp"):
        mine = exact(vec)
        vec = joined(mine) + joined(swap(mine, "dp", distance))
        distance *= 2
    return vec


def rotary_tables(rot_dims):
    position = jnp.arange(SEQ).astype(F32)
    inverse = 1.0 / 10000.0 ** (jnp.arange(0, rot_dims, 2).astype(F32) / rot_dims)
    angles = inverse[:, None] * position[None, :]
    return jnp.cos(angles), jnp.sin(angles)


def tied(values, *others):
    return lax.optimization_barrier((values, others))[0]


def body(
    tokens, cotangent, attention_norm_gain, attention_norm_bias, feedforward_norm_gain, feedforward_norm_bias,
    w_qkv, bias_qv, bias_key, w_dense, bias_dense, w_fc1, bias_fc1, w_fc2, bias_fc2,
):
    width = tokens.shape[1]
    rot_dims = bias_key.shape[1]
    core = bit_of("dp", 1)
    bits = jnp.stack([core, bit_of("tensor", 1), spot()]).astype(jnp.int32)

    x_far = swap(tokens, "tensor", 1)

    wa = jnp.concatenate([w_qkv.transpose(1, 2, 0).reshape(-1, width), w_dense], 0)
    key_bias = jnp.pad(bias_key, ((0, 0), (0, 64 - rot_dims))).reshape(192)
    bias = jnp.stack([jnp.concatenate([bias_qv[0], key_bias, bias_qv[1], jnp.zeros((192,), F32)]), bias_fc1])
    at = (4 * core + spot()) * 96
    pieces = jnp.concatenate([lax.dynamic_slice_in_dim(w, at, 96, 0) for w in (w_fc1, w_fc2, wa)], 0)
    pieces_far = swap(pieces, "tensor", 2)
    bias_far = swap(bias, "tensor", 2)
    rotary = rotary_tables(rot_dims)
    pad8 = lambda row: jnp.broadcast_to(row[None], (8, width))
    norms = jnp.stack([attention_norm_gain, attention_norm_bias, feedforward_norm_gain, feedforward_norm_bias])

    b1 = pad8(bias[1])
    mlp_out, dn2, db, g1, g2 = mlp_half(True, tokens, norms, cotangent, w_fc1, w_fc2, b1)
    x_far = tied(x_far, g1)
    dy_far = swap(tied(cotangent, x_far), "tensor", 1)

    x_far, pieces_far, bias_far = tied((x_far, pieces_far, bias_far), pieces_far, bias_far)
    got = exchange([pieces_far] * 3)
    n1, *saved, ot = attn_forward(True, bits, tokens, x_far, norms, wa, pad8(bias[0]), *rotary)
    dy_far, ot = tied((dy_far, ot), dy_far)
    mlp_out_far, dn2_far, db, keep, send = mlp_half(
        False, tied(x_far, ot), norms, dy_far, w_fc1, w_fc2, b1, bits, db, *near((g1, g2))
    )
    keep, send, got = tied((keep, send, got), got)
    send_far = swap(send, "dp", 1)
    mine = [pieces_far, *got]
    theirs = core_swap(mine)
    fc_own, sent = messages(keep, send_far)
    fc_got = exchange(sent)

    mlp_out, dn2, mlp_out_far, dn2_far, db_far, keep, send, wa_far = mlp_other(
        *mine, *theirs, bits, pad8(bias_far[1]), norms, tokens, cotangent, x_far, dy_far,
        *away((mlp_out, tied(dn2, sent), mlp_out_far, dn2_far)),
    )
    keep, send, wa_far, fc_got = tied((keep, send, wa_far, fc_got), fc_got)
    send_far = swap(send, "dp", 1)
    fc_far, sent = messages(keep, send_far)
    got = exchange(sent)
    n1, wa_far, ot = away((n1, tied(wa_far, sent), ot))
    *saved_far, out_keep, out_send = attn_forward(
        False, bits, n1, wa_far, pad8(bias_far[0]), *rotary, ot, w_dense, *away((mlp_out, mlp_out_far)),
    )
    out_send, saved_far, got = tied((out_send, saved_far, got), got)
    fc_far = summed(fc_far, got).astype(BF)
    fc_far_in = swap(fc_far, "tensor", 2)
    out_far = swap(tied(out_send, fc_far), "tensor", 1)
    qkv, kt, lse, ot_far = tied(saved_far, fc_far)
    keep, send, dn1 = attn_backward(
        False, bits, near(qkv), near(kt), lse, near(ot_far), n1, cotangent, dy_far, wa_far, *rotary, db_far
    )
    keep, send, dn1, fc_far_in = tied((keep, send, dn1, fc_far_in), fc_far_in)
    send_far = swap(send, "dp", 1)
    vec_far = joined(send[384:]) + joined(send_far[384:])
    a_far, sent = messages(keep[None], send_far[None, :384], vec_far)
    fc_own = summed(fc_own, fc_got)
    fc_grad = lax.reduce_precision(far_sum(fc_own + fc_far_in.astype(F32)), 8, 7).astype(BF).reshape(192, width)
    sent = [jnp.concatenate([message, fc_grad], 0) for message in sent]
    got = exchange(sent)
    keep, send, e_keep, e_send = attn_backward(
        True, bits, *away((*saved, ot)), n1, cotangent, dy_far, wa, *rotary, db, near(tied(dn1, sent)),
        *away((dn2, dn2_far)), tokens, x_far, norms,
    )
    keep, send, e_keep, e_send, got, out_far = tied((keep, send, e_keep, e_send, got, out_far), got, out_far)

    send_far = swap(send, "dp", 1)
    vec_raw = send[384:]
    vec_pair = swap(vec_raw, "tensor", 1)
    fc_mine = jnp.stack([fc_grad, *(message[112:] for message in got)])
    fc_theirs = swap(fc_mine, "dp", 1)
    a_far, vec_far = summed(a_far, [message[:112] for message in got], vec_far)
    far_send = jnp.concatenate([a_far[0].astype(BF), exact(vec_far)], 0)
    far = swap(far_send, "tensor", 2)
    e_far = swap(e_send, "tensor", 1)
    shared = lax.broadcasted_iota(jnp.int32, (8, 1), 0) >= 2
    vec = joined(vec_raw) + jnp.where(shared, joined(vec_pair), 0.0)
    keep = tied(keep, fc_theirs, vec_pair)
    a_own, sent = messages(keep[None], send_far[None, :384], vec)
    a_got = exchange(sent)
    fc1_grad, fc2_grad = finish(2, bits, fc_mine, tied(fc_theirs, sent))
    own_tokens = tokens.astype(F32)
    mixed_out = (own_tokens + (out_keep + tied(out_far, sent).astype(F32)) + bias_dense + bias_fc2).astype(BF)
    a_own, vec = summed(a_own, tied(a_got, mixed_out, fc1_grad), vec)
    a_grad = lax.reduce_precision(far_sum(a_own + far[None, :96].astype(F32)), 8, 7).astype(BF).reshape(96, width)
    a_got = exchange([a_grad] * 3)
    packet = exact(tied(vec, a_grad))
    vec = far_sum_exact(joined(packet) + joined(swap(packet, "dp", 1)))
    quarter_vec = vec + joined(far[96:])
    packet = exact(vec)
    e_far = tied(e_far, packet)
    vec = joined(packet) + joined(swap(packet, "tensor", 2))

    e = e_keep + e_far.astype(F32)
    centered = own_tokens - jnp.mean(own_tokens, axis=-1, keepdims=True)
    r = lax.rsqrt(jnp.mean(centered * centered, axis=-1, keepdims=True) + EPS)
    xhat = centered * r
    dx = r * (e - jnp.mean(e, axis=-1, keepdims=True) - xhat * jnp.mean(e * xhat, axis=-1, keepdims=True))
    grad_tokens = (cotangent.astype(F32) + dx).astype(BF)

    mine = jnp.stack(tied([a_grad, *a_got], vec))
    qkv_grad, dense_grad = finish(1, bits, mine, swap(mine, "dp", 1))
    columns = quarter_vec[1]
    return (
        mixed_out,
        grad_tokens,
        vec[2],
        vec[3],
        vec[4],
        vec[5],
        qkv_grad.reshape(3, 192, width).transpose(2, 0, 1),
        jnp.stack([columns[:192], columns[384:576]]),
        columns[192:384].reshape(3, 64)[:, :rot_dims],
        dense_grad,
        vec[6],
        fc1_grad,
        quarter_vec[0],
        fc2_grad,
        vec[6],
    )


def solution(mesh):
    rows = P(("dp", "tensor"), None)
    in_specs = (
        rows, rows, P(), P(), P(), P(), P(None, None, "tensor"), P(None, "tensor"), P("tensor", None),
        P("tensor", None), P(), P(None, "tensor"), P("tensor"), P("tensor", None), P(),
    )
    out_specs = (
        rows, rows, P(), P(), P(), P(), P(None, None, "tensor"), P(None, "tensor"), P("tensor", None),
        P("tensor", None), P(), P(None, "tensor"), P("tensor"), P("tensor", None), P(),
    )
    return jax.shard_map(body, mesh=mesh, in_specs=in_specs, out_specs=out_specs, check_vma=False)
```

```python
import math

import jax
import jax.numpy as jnp
from jax import lax
from jax.experimental import pallas as pl
from jax.experimental.pallas import tpu as pltpu
from jax.sharding import PartitionSpec as P

SEQ = 1024
EPS = 1e-05
BF = jnp.bfloat16
F32 = jnp.float32
BQ = 512
NB = SEQ // BQ
HALF = SEQ // 2


def nn(a, b):
    return lax.dot_general(a, b, (((1,), (0,)), ((), ())), preferred_element_type=F32)


def nt(a, b):
    return lax.dot_general(a, b, (((1,), (1,)), ((), ())), preferred_element_type=F32)


def call(kernel, name, args, outs, scratch=(), flops=0, transcendentals=0, limit=28):
    moved = sum(a.size * a.dtype.itemsize for a in args) + sum(math.prod(o[0]) * jnp.dtype(o[1]).itemsize for o in outs)
    spaces = [pltpu.SMEM if a.dtype == jnp.int32 else pltpu.VMEM for a in args]
    return pl.pallas_call(
        kernel,
        in_specs=[pl.BlockSpec(memory_space=s) for s in spaces],
        out_specs=[pl.BlockSpec(memory_space=pltpu.VMEM)] * len(outs),
        out_shape=[(pltpu.VMEM if stays else pltpu.HBM)(s, d) for s, d, stays in outs],
        scratch_shapes=[pltpu.VMEM(s, d) for s, d in scratch],
        compiler_params=pltpu.CompilerParams(vmem_limit_bytes=limit * 2**20),
        cost_estimate=pl.CostEstimate(flops=flops, bytes_accessed=moved, transcendentals=transcendentals),
        name=name,
    )(*args)


def near(values):
    return jax.tree.map(lambda v: pltpu.with_memory_space_constraint(v, pltpu.VMEM), values)


def away(values):
    return jax.tree.map(lambda v: pltpu.with_memory_space_constraint(v, pltpu.HBM), values)


def own_rows(bits_ref):
    half = bits_ref[1]
    return pl.ds(pl.multiple_of(HALF * half, HALF), HALF), pl.ds(pl.multiple_of(HALF - HALF * half, HALF), HALF)


def place_strips(bits_ref, mine, theirs, put):
    for slot in range(4):
        at = 96 * (bits_ref[2] ^ slot)
        put(pl.multiple_of(384 * bits_ref[0] + at, 96), mine[slot])
        put(pl.multiple_of(384 - 384 * bits_ref[0] + at, 96), theirs[slot])


def normalized(x_ref, gain, shift, put):
    for i in range(HALF // BQ):
        rows = pl.ds(i * BQ, BQ)
        x = x_ref[rows, :].astype(F32)
        centered = x - jnp.mean(x, axis=-1, keepdims=True)
        r = lax.rsqrt(jnp.mean(centered * centered, axis=-1, keepdims=True) + EPS)
        put(i * BQ, centered * r * gain + shift)


def tile(i):
    return slice(128 * i, 128 * (i + 1))


HEADS = ((0, 0, 1, 2, 0), (0, 1, 1, 2, 1), (4, 0, 5, 4, 1))
TILES = {0: (0, 64), 1: (192, 256), 2: (384, 448), 4: (128, 512), 5: (320, None)}
ROTATED = (0, 64, 128, 192, 256, 320)


def masked(x, half):
    keep = lax.broadcasted_iota(jnp.int32, x.shape, 1) < 64
    zero = jnp.zeros_like(x)
    return jnp.where(keep, x, zero) if half == 0 else jnp.where(keep, zero, x)


def causal(x, fill):
    rows = lax.broadcasted_iota(jnp.int32, x.shape, 0)
    cols = lax.broadcasted_iota(jnp.int32, x.shape, 1)
    return jnp.where(rows <= cols, x, fill)


def attn_forward_kernel(first, *refs):
    if first:
        bits_ref, x_ref, x_far_ref, norm_ref, w_ref, bias_ref, cos_ref, sin_ref = refs[:8]
        n_ref, qkv_ref, kt_ref, lse_ref, ot_ref, m_ref, o_ref, vt_ref = refs[8:]
        for x, at in ((x_ref, HALF * bits_ref[1]), (x_far_ref, HALF - HALF * bits_ref[1])):
            def put(row, n):
                n_ref[pl.ds(pl.multiple_of(at + row, BQ), BQ), :] = n.astype(BF)

            normalized(x, norm_ref[0:1], norm_ref[1:2], put)
    else:
        bits_ref, n_ref, w_ref, bias_ref, cos_ref, sin_ref, ot_in_ref, wd_in_ref, mlp_ref, mlp_far_ref = refs[:10]
        qkv_ref, kt_ref, lse_ref, ot_ref, keep_ref, send_ref, m_ref, o_ref, vt_ref, out_ref = refs[10:]
    n = n_ref[...]
    bias = bias_ref[...].T
    for at, size in ((0, 256), (256, 320)):
        m_ref[pl.ds(at, size), :] = nt(w_ref[pl.ds(at, size), :], n) + bias[at : at + size, 0:1]
    cos, sin = cos_ref[...], sin_ref[...]
    for at in ROTATED:
        one, two = m_ref[pl.ds(at, 8), :], m_ref[pl.ds(at + 8, 8), :]
        m_ref[pl.ds(at, 8), :] = one * cos - two * sin
        m_ref[pl.ds(at + 8, 8), :] = two * cos + one * sin
    m_ref[pl.ds(0, 192), :] = m_ref[pl.ds(0, 192), :] * 0.125
    for i, (one, two) in TILES.items():
        upper = jnp.zeros((64, SEQ), F32) if two is None else m_ref[pl.ds(two, 64), :]
        qkv_ref[:, tile(i)] = jnp.concatenate([m_ref[pl.ds(one, 64), :], upper], 0).T.astype(BF)
    kt_ref[...] = m_ref[pl.ds(192, 192), :].astype(BF)
    vt_ref[...] = m_ref[pl.ds(384, 192), :].astype(BF)

    lse_ref[...] = jnp.zeros((8, SEQ), F32)
    for h, (qt, qh, kt, vt, vh) in enumerate(HEADS):
        v_rows = pl.ds(64 * h, 64)
        for j in range(NB):
            cols = pl.ds(j * BQ, BQ)
            past = pl.ds(0, j * BQ)
            q = masked(qkv_ref[cols, tile(qt)], qh)
            st_d = causal(nt(qkv_ref[cols, tile(kt)], q), -1e30)
            top = jnp.max(st_d, axis=0, keepdims=True)
            if j:
                st = nt(qkv_ref[past, tile(kt)], q)
                top = jnp.maximum(top, jnp.max(st, axis=0, keepdims=True))
            w_d = jnp.exp(st_d - top)
            total = jnp.sum(w_d, axis=0, keepdims=True)
            o = nn(vt_ref[v_rows, cols], w_d.astype(BF))
            if j:
                w = jnp.exp(st - top)
                total = total + jnp.sum(w, axis=0, keepdims=True)
                o = o + nn(vt_ref[v_rows, past], w.astype(BF))
            o_ref[pl.ds(64 * h, 64), cols] = o * (1.0 / total)
            lse_ref[pl.ds(h, 1), cols] = top + jnp.log(total)
    ot_ref[...] = o_ref[...].astype(BF)
    if not first:
        own, far = own_rows(bits_ref)
        out_ref[...] = nn(o_ref[...].T.astype(BF), w_ref[pl.ds(576, 192), :]) + nn(
            ot_in_ref[...].astype(F32).T.astype(BF), wd_in_ref[...]
        )
        keep_ref[...] = out_ref[own, :] + mlp_ref[...].astype(F32)
        send_ref[...] = (out_ref[far, :] + mlp_far_ref[...].astype(F32)).astype(BF)


def attn_forward(first, *args):
    outs = [
        ((SEQ, 768), BF, False),
        ((SEQ, 768), BF, not first),
        ((192, SEQ), BF, not first),
        ((8, SEQ), F32, False),
        ((192, SEQ), BF, not first),
    ]
    scratch = [((576, SEQ), F32), ((192, SEQ), F32), ((192, SEQ), BF)]
    if not first:
        outs = outs[1:] + [((HALF, 768), F32, False), ((HALF, 768), BF, False)]
        scratch.append(((SEQ, 768), F32))
    kernel = lambda *refs: attn_forward_kernel(first, *refs)
    return call(kernel, "attn_forward", args, outs, scratch, 4 * 10**9, 2 * 10**6)


def normal_cdf(hidden):
    return 0.5 * (1.0 + lax.erf(hidden * math.sqrt(0.5)))


def mlp_hidden(n_ref, dy_ref, w1_ref, w2_ref, bias_ref, a_ref, dh_ref, db_ref):
    dy = dy_ref[...]
    for i in range(3):
        cols = slice(256 * i, 256 * (i + 1))
        hidden = nn(n_ref[...], w1_ref[:, cols]) + bias_ref[0:1, cols]
        cdf = normal_cdf(hidden)
        a_ref[:, cols] = (hidden * cdf).astype(BF)
        slope = cdf + hidden * (jnp.exp(-0.5 * hidden * hidden) * (1.0 / math.sqrt(2.0 * math.pi)))
        dh = (nt(dy, w2_ref[cols, :]) * slope).astype(BF)
        dh_ref[:, cols] = dh
        db_ref[:, cols] = jnp.broadcast_to(jnp.sum(dh.astype(F32), axis=0, keepdims=True), (8, 256))


def split_gradients(bits_ref, grads, keep_ref, send_ref):
    core = bits_ref[0]
    for i, g in enumerate(grads):
        keep_ref[i] = g[pl.ds(pl.multiple_of(384 * core, 384), 384), :].astype(BF)
        send_ref[i] = g[pl.ds(pl.multiple_of(384 - 384 * core, 384), 384), :].astype(BF)


def second_norm(x_ref, norm_ref, n_ref, nt_ref, at=0):
    def put(row, n):
        n_ref[pl.ds(at + row, BQ), :] = n.astype(BF)
        nt_ref[:, pl.ds(at + row, BQ)] = n.T.astype(BF)

    normalized(x_ref, norm_ref[2:3], norm_ref[3:4], put)


def mlp_half_kernel(first, *refs):
    if first:
        x_ref, norm_ref, dy_ref, w1_ref, w2_ref, bias_ref = refs[:6]
        out_ref, dn_ref, db_ref, g1_ref, g2_ref, n_ref, nt_ref, a_ref, dh_ref = refs[6:]
    else:
        x_ref, norm_ref, dy_ref, w1_ref, w2_ref, bias_ref, bits_ref, db_in_ref, g1_in_ref, g2_in_ref = refs[:10]
        out_ref, dn_ref, db_ref, keep_ref, send_ref, n_ref, nt_ref, a_ref, dh_ref, g1_ref, g2_ref = refs[10:]
    second_norm(x_ref, norm_ref, n_ref, nt_ref)
    mlp_hidden(n_ref, dy_ref, w1_ref, w2_ref, bias_ref, a_ref, dh_ref, db_ref)
    g1, g2 = nn(nt_ref[...], dh_ref[...]), nn(a_ref[...].T, dy_ref[...])
    g1_ref[...] = g1 if first else g1 + g1_in_ref[...]
    g2_ref[...] = g2 if first else g2 + g2_in_ref[...]
    out_ref[...] = nn(a_ref[...], w2_ref[...]).astype(BF)
    dn_ref[...] = nt(dh_ref[...], w1_ref[...]).astype(BF)
    if not first:
        db_ref[...] += db_in_ref[...]
        split_gradients(bits_ref, (g1_ref, g2_ref), keep_ref, send_ref)


SPLIT_OUTS = [((2, 384, 768), BF, False)] * 2


def mlp_half(first, *args):
    grads = [((768, 768), F32, True)] * 2
    outs = [((HALF, 768), BF, False)] * 2 + [((8, 768), F32, False)] + (grads if first else SPLIT_OUTS)
    scratch = [((HALF, 768), BF), ((768, HALF), BF), ((HALF, 768), BF), ((HALF, 768), BF)] + ([] if first else [g[:2] for g in grads])
    kernel = lambda *refs: mlp_half_kernel(first, *refs)
    return call(kernel, "mlp_half", args, outs, scratch, 36 * 10**8, 10**6)


def mlp_other_kernel(*refs):
    mine, theirs, refs = refs[:4], refs[4:8], refs[8:]
    bits_ref, bias_ref, norm_ref, x_ref, dy_ref, x_far_ref, dy_far_ref = refs[:7]
    refs = refs[7:]
    before, after = refs[:4], refs[4:8]
    db_ref, keep_ref, send_ref, wa_ref, n_ref, nt_ref, dy_all_ref, a_ref, dh_ref = refs[8:17]
    g1_ref, g2_ref, w1_ref, w2_ref = refs[17:]
    second_norm(x_ref, norm_ref, n_ref, nt_ref)
    second_norm(x_far_ref, norm_ref, n_ref, nt_ref, HALF)
    dy_all_ref[pl.ds(0, HALF), :] = dy_ref[...]
    dy_all_ref[pl.ds(HALF, HALF), :] = dy_far_ref[...]

    def put(row, ref):
        for i, w in enumerate((w1_ref, w2_ref, wa_ref)):
            w[pl.ds(row, 96), :] = ref[pl.ds(96 * i, 96), :]

    place_strips(bits_ref, mine, theirs, put)
    mlp_hidden(n_ref, dy_all_ref, w1_ref, w2_ref, bias_ref, a_ref, dh_ref, db_ref)
    g1_ref[...] = nn(nt_ref[...], dh_ref[...])
    g2_ref[...] = nn(a_ref[...].T, dy_all_ref[...])
    for half in range(2):
        rows = pl.ds(HALF * half, HALF)
        old, new = before[2 * half : 2 * half + 2], after[2 * half : 2 * half + 2]
        new[0][...] = (nn(a_ref[rows, :], w2_ref[...]) + old[0][...].astype(F32)).astype(BF)
        new[1][...] = (nt(dh_ref[rows, :], w1_ref[...]) + old[1][...].astype(F32)).astype(BF)
    split_gradients(bits_ref, (g1_ref, g2_ref), keep_ref, send_ref)


def mlp_other(*args):
    outs = [((HALF, 768), BF, False)] * 4
    outs += [((8, 768), F32, False)] + SPLIT_OUTS + [((768, 768), BF, False)]
    scratch = [((SEQ, 768), BF), ((768, SEQ), BF)] + [((SEQ, 768), BF)] * 3 + [((768, 768), F32)] * 2 + [((768, 768), BF)] * 2
    return call(mlp_other_kernel, "mlp_other", args, outs, scratch, 72 * 10**8, 2 * 10**6, 40)


def finish_kernel(kinds, bits_ref, *refs):
    mine, theirs = ([ref.at[slot] for slot in range(4)] for ref in refs[:2])
    outs = refs[2:]
    full = outs if kinds == 2 else outs[2:]

    def put(row, ref):
        for i, out in enumerate(full):
            out[pl.ds(row, 96), :] = ref[pl.ds(96 * i, 96), :].astype(F32)

    place_strips(bits_ref, mine, theirs, put)
    if kinds == 1:
        outs[0][...] = full[0][pl.ds(0, 576), :]
        outs[1][...] = full[0][pl.ds(576, 192), :]


def finish(kinds, bits, mine, theirs):
    shapes = [(768, 768), (768, 768)] if kinds == 2 else [(576, 768), (192, 768)]
    kernel = lambda *refs: finish_kernel(kinds, *refs)
    scratch = [] if kinds == 2 else [((768, 768), F32)]
    return call(kernel, "finish", (bits, mine, theirs), [(s, F32, False) for s in shapes], scratch)


def attn_backward_kernel(last, *refs):
    bits_ref, qkv_ref, kt_ref, lse_ref, ot_ref, n_ref, dy_own_ref, dy_far_ref, w_ref, cos_ref, sin_ref, db_ref = refs[:12]
    if last:
        in_ref, dn2_ref, dn2_far_ref, x_ref, x_far_ref, norm_ref = refs[12:18]
        keep_ref, send_ref, e_keep_ref, e_send_ref, raw_ref = refs[18:23]
        dn_ref = refs[-8]
    else:
        keep_ref, send_ref, dn_ref = refs[12:15]
    dy_ref, do_ref, dk_ref, dv_ref, dt_ref, d_ref, g_ref = refs[-7:]
    own, far = own_rows(bits_ref)
    dy_ref[own, :] = dy_own_ref[...]
    dy_ref[far, :] = dy_far_ref[...]
    dy = dy_ref[...]
    do_ref[0] = nt(dy, w_ref[pl.ds(576, 128), :]).astype(BF)
    do_ref[1] = nt(dy, w_ref[pl.ds(640, 128), :]).astype(BF)
    dk_ref[...] = jnp.zeros_like(dk_ref)
    dv_ref[...] = jnp.zeros_like(dv_ref)
    for h, (qt, qh, kt, vt, vh) in enumerate(HEADS):
        a = h // 2
        rows = pl.ds(64 * h, 64)
        for j in range(NB):
            cols = pl.ds(j * BQ, BQ)
            past = pl.ds(0, j * BQ)
            q = masked(qkv_ref[cols, tile(qt)], qh)
            do = masked(do_ref[a, cols, :], vh)
            lse = lse_ref[pl.ds(h, 1), cols]
            p_d = jnp.exp(causal(nt(qkv_ref[cols, tile(kt)], q), -1e30) - lse)
            dp_d = nt(qkv_ref[cols, tile(vt)], do)
            delta = jnp.sum(p_d * dp_d, axis=0, keepdims=True)
            if j:
                p = jnp.exp(nt(qkv_ref[past, tile(kt)], q) - lse)
                dp = nt(qkv_ref[past, tile(vt)], do)
                delta = delta + jnp.sum(p * dp, axis=0, keepdims=True)
            ds_d = (p_d * (dp_d - delta)).astype(BF)
            dv_ref[a, cols, :] += nn(p_d.astype(BF), do)
            dk_ref[a, cols, :] += nn(ds_d, q)
            dqt = nn(kt_ref[rows, cols], ds_d)
            if j:
                ds = (p * (dp - delta)).astype(BF)
                dv_ref[a, past, :] += nn(p.astype(BF), do)
                dk_ref[a, past, :] += nn(ds, q)
                dqt = dqt + nn(kt_ref[rows, past], ds)
            dt_ref[rows, cols] = dqt * 0.125
    dt_ref[pl.ds(192, 128), :] = dk_ref[0].T
    dt_ref[pl.ds(320, 64), :] = dk_ref[1].T[:64]
    dt_ref[pl.ds(384, 128), :] = dv_ref[0].T
    dt_ref[pl.ds(512, 64), :] = dv_ref[1].T[64:]
    dt_ref[pl.ds(576, 64), :] = jnp.zeros((64, SEQ), F32)
    cos, sin = cos_ref[...], sin_ref[...]
    for at in ROTATED:
        one, two = dt_ref[pl.ds(at, 8), :], dt_ref[pl.ds(at + 8, 8), :]
        dt_ref[pl.ds(at, 8), :] = one * cos + two * sin
        dt_ref[pl.ds(at + 8, 8), :] = two * cos - one * sin
    for i in range(5):
        d_ref[:, tile(i)] = dt_ref[tile(i), :].T.astype(BF)
    d = d_ref[...]
    g_ref[pl.ds(0, 576), :] = nn(dt_ref[pl.ds(0, 576), :].astype(BF), n_ref[...])
    g_ref[pl.ds(576, 192), :] = nn(ot_ref[...], dy)
    dn = nn(d, w_ref[pl.ds(0, 640), :])

    core = bits_ref[0]
    keep_ref[...] = g_ref[pl.ds(pl.multiple_of(384 * core, 384), 384), :].astype(BF)
    send_ref[pl.ds(0, 384), :] = g_ref[pl.ds(pl.multiple_of(384 - 384 * core, 384), 384), :].astype(BF)
    row = lax.broadcasted_iota(jnp.int32, (8, 768), 0)
    columns = jnp.concatenate([nn(jnp.ones((8, SEQ), BF), d), jnp.zeros((8, 128), F32)], 1)
    vec = jnp.where(row == 0, db_ref[...], jnp.where(row == 1, columns, 0.0))
    if last:
        dn_ref[...] = dn + in_ref[...]
        gain1, gain2 = norm_ref[0:1], norm_ref[2:3]
        sums = [0.0] * 4
        for rows, dn2_rows, x_rows in ((own, dn2_ref, x_ref), (far, dn2_far_ref, x_far_ref)):
            dn1, dn2, x = dn_ref[rows, :], dn2_rows[...].astype(F32), x_rows[...].astype(F32)
            e = dn1 * gain1 + dn2 * gain2
            if rows is own:
                e_keep_ref[...] = e
            else:
                e_send_ref[...] = e.astype(BF)
            centered = x - jnp.mean(x, axis=-1, keepdims=True)
            xhat = centered * lax.rsqrt(jnp.mean(centered * centered, axis=-1, keepdims=True) + EPS)
            for i, term in enumerate((dn1 * xhat, dn1, dn2 * xhat, dn2)):
                sums[i] = sums[i] + jnp.sum(term, axis=0, keepdims=True)
        sums.append(jnp.sum(dy_own_ref[...].astype(F32), axis=0, keepdims=True))
        for i, value in enumerate(sums):
            vec = jnp.where(row == 2 + i, value, vec)
    else:
        dn_ref[...] = dn
    high = vec.astype(BF)
    raw = jnp.concatenate([high, (vec - high.astype(F32)).astype(BF)], 0)
    send_ref[pl.ds(384, 16), :] = raw
    if last:
        raw_ref[...] = raw


def attn_backward(last, *args):
    outs = [((384, 768), BF, False), ((400, 768), BF, False)]
    if last:
        outs += [((HALF, 768), F32, False), ((HALF, 768), BF, False), ((16, 768), BF, False)]
    else:
        outs += [((SEQ, 768), F32, True)]
    scratch = [
        ((SEQ, 768), BF),
        ((2, SEQ, 128), BF),
        ((2, SEQ, 128), F32),
        ((2, SEQ, 128), F32),
        ((640, SEQ), F32),
        ((SEQ, 640), BF),
        ((768, 768), F32),
    ]
    if last:
        scratch.insert(0, ((SEQ, 768), F32))
    kernel = lambda *refs: attn_backward_kernel(last, *refs)
    return call(kernel, "attn_backward", args, outs, scratch, 5 * 10**9, 10**6, 40)


def swap(value, axis, distance):
    size = lax.axis_size(axis)
    return lax.ppermute(value, axis, [(i, i ^ distance) for i in range(size)])


def bit_of(axis, distance):
    return (lax.axis_index(axis) // distance) % 2


def exact(vec):
    high = lax.reduce_precision(vec, 8, 7)
    return jnp.concatenate([high.astype(BF), (vec - high).astype(BF)], 0)


def joined(pair):
    rows = pair.shape[0] // 2
    return pair[:rows].astype(F32) + pair[rows:].astype(F32)


def spot():
    return 2 * bit_of("dp", 2) + bit_of("dp", 4)


PEERS = ((4, 1), (2, 2), (6, 3))


def messages(keep, got, vec=None):
    def part(change):
        at = (spot() ^ change) * 96
        cut = lambda v: lax.dynamic_slice_in_dim(v, at, 96, 1).astype(F32)
        return cut(keep) + cut(got)

    out = []
    for _, change in PEERS:
        sent = part(change).astype(BF).reshape(-1, keep.shape[-1])
        out.append(sent if vec is None else jnp.concatenate([sent, exact(vec)], 0))
    return part(0), out


def exchange(out):
    return [swap(message, "dp", distance) for (distance, _), message in zip(PEERS, out)]


def summed(own, got, vec=None):
    rows = own.shape[0] * 96
    total = own
    for message in got:
        total = total + message[:rows].reshape(own.shape).astype(F32)
    if vec is None:
        return total
    y, x, both = (joined(message[rows:]) for message in got)
    return total, (joined(exact(vec)) + y) + (x + both)


def core_swap(parts):
    return [swap(part, "dp", 1) for part in parts]


def far_sum(value):
    distance = 8
    while distance < lax.axis_size("dp"):
        mine = lax.reduce_precision(value, 8, 7)
        value = mine + swap(mine.astype(BF), "dp", distance).astype(F32)
        distance *= 2
    return value


def far_sum_exact(vec):
    distance = 8
    while distance < lax.axis_size("dp"):
        mine = exact(vec)
        vec = joined(mine) + joined(swap(mine, "dp", distance))
        distance *= 2
    return vec


def rotary_tables(rot_dims):
    position = jnp.arange(SEQ).astype(F32)
    inverse = 1.0 / 10000.0 ** (jnp.arange(0, rot_dims, 2).astype(F32) / rot_dims)
    angles = inverse[:, None] * position[None, :]
    return jnp.cos(angles), jnp.sin(angles)


def tied(values, *others):
    return lax.optimization_barrier((values, others))[0]


def body(
    tokens, cotangent, attention_norm_gain, attention_norm_bias, feedforward_norm_gain, feedforward_norm_bias,
    w_qkv, bias_qv, bias_key, w_dense, bias_dense, w_fc1, bias_fc1, w_fc2, bias_fc2,
):
    width = tokens.shape[1]
    rot_dims = bias_key.shape[1]
    core = bit_of("dp", 1)
    bits = jnp.stack([core, bit_of("tensor", 1), spot()]).astype(jnp.int32)

    x_far = swap(tokens, "tensor", 1)

    wa = jnp.concatenate([w_qkv.transpose(1, 2, 0).reshape(-1, width), w_dense], 0)
    key_bias = jnp.pad(bias_key, ((0, 0), (0, 64 - rot_dims))).reshape(192)
    bias = jnp.stack([jnp.concatenate([bias_qv[0], key_bias, bias_qv[1], jnp.zeros((192,), F32)]), bias_fc1])
    at = (4 * core + spot()) * 96
    pieces = jnp.concatenate([lax.dynamic_slice_in_dim(w, at, 96, 0) for w in (w_fc1, w_fc2, wa)], 0)
    pieces_far = swap(pieces, "tensor", 2)
    bias_far = swap(bias, "tensor", 2)
    rotary = rotary_tables(rot_dims)
    pad8 = lambda row: jnp.broadcast_to(row[None], (8, width))
    norms = jnp.stack([attention_norm_gain, attention_norm_bias, feedforward_norm_gain, feedforward_norm_bias])

    b1 = pad8(bias[1])
    mlp_out, dn2, db, g1, g2 = mlp_half(True, tokens, norms, cotangent, w_fc1, w_fc2, b1)
    x_far = tied(x_far, g1)
    dy_far = swap(tied(cotangent, x_far), "tensor", 1)

    pieces_far = tied(pieces_far, x_far)
    x_far, bias_far = tied((x_far, bias_far), pieces_far, bias_far)
    got = exchange([pieces_far] * 3)
    n1, *saved, ot = attn_forward(True, bits, tokens, x_far, norms, wa, pad8(bias[0]), *rotary)
    dy_far, ot = tied((dy_far, ot), dy_far)
    mlp_out_far, dn2_far, db, keep, send = mlp_half(
        False, tied(x_far, ot), norms, dy_far, w_fc1, w_fc2, b1, bits, db, *near((g1, g2))
    )
    keep, send, got = tied((keep, send, got), got)
    send_far = swap(send, "dp", 1)
    mine = [pieces_far, *got]
    theirs = core_swap(mine)
    fc_own, sent = messages(keep, send_far)
    fc_got = exchange(sent)

    mlp_out, dn2, mlp_out_far, dn2_far, db_far, keep, send, wa_far = mlp_other(
        *mine, *theirs, bits, pad8(bias_far[1]), norms, tokens, cotangent, x_far, dy_far,
        *away((mlp_out, tied(dn2, sent), mlp_out_far, dn2_far)),
    )
    keep, send, wa_far, fc_got = tied((keep, send, wa_far, fc_got), fc_got)
    send_far = swap(send, "dp", 1)
    fc_far, sent = messages(keep, send_far)
    got = exchange(sent)
    n1, wa_far, ot = away((n1, tied(wa_far, sent), ot))
    *saved_far, out_keep, out_send = attn_forward(
        False, bits, n1, wa_far, pad8(bias_far[0]), *rotary, ot, w_dense, *away((mlp_out, mlp_out_far)),
    )
    out_send, saved_far, got = tied((out_send, saved_far, got), got)
    fc_far = summed(fc_far, got).astype(BF)
    fc_far_in = swap(fc_far, "tensor", 2)
    out_far = swap(tied(out_send, fc_far), "tensor", 1)
    qkv, kt, lse, ot_far = tied(saved_far, fc_far)
    keep, send, dn1 = attn_backward(
        False, bits, near(qkv), near(kt), lse, near(ot_far), n1, cotangent, dy_far, wa_far, *rotary, db_far
    )
    keep, send, dn1, fc_far_in = tied((keep, send, dn1, fc_far_in), fc_far_in)
    send_far = swap(send, "dp", 1)
    vec_far = joined(send[384:]) + joined(send_far[384:])
    a_far, sent = messages(keep[None], send_far[None, :384], vec_far)
    fc_own = summed(fc_own, fc_got)
    fc_grad = lax.reduce_precision(far_sum(fc_own + fc_far_in.astype(F32)), 8, 7).astype(BF).reshape(192, width)
    sent = [jnp.concatenate([message, fc_grad], 0) for message in sent]
    got = exchange(sent)
    keep, send, e_keep, e_send, vec_raw = attn_backward(
        True, bits, *away((*saved, ot)), n1, cotangent, dy_far, wa, *rotary, db, near(tied(dn1, sent)),
        *away((dn2, dn2_far)), tokens, x_far, norms,
    )
    keep, send, e_keep, e_send, vec_raw, got, out_far = tied(
        (keep, send, e_keep, e_send, vec_raw, got, out_far), got, out_far
    )

    send_far = swap(send, "dp", 1)
    vec_pair = swap(vec_raw, "tensor", 1)
    fc_mine = jnp.stack([fc_grad, *(message[112:] for message in got)])
    fc_theirs = swap(fc_mine, "dp", 1)
    a_far, vec_far = summed(a_far, [message[:112] for message in got], vec_far)
    far_send = jnp.concatenate([a_far[0].astype(BF), exact(vec_far)], 0)
    far = swap(far_send, "tensor", 2)
    e_far = swap(e_send, "tensor", 1)
    shared = lax.broadcasted_iota(jnp.int32, (8, 1), 0) >= 2
    vec = joined(vec_raw) + jnp.where(shared, joined(vec_pair), 0.0)
    keep = tied(keep, fc_theirs, vec_pair)
    a_own, sent = messages(keep[None], send_far[None, :384], vec)
    a_got = exchange(sent)
    fc1_grad, fc2_grad = finish(2, bits, fc_mine, tied(fc_theirs, sent))
    own_tokens = tokens.astype(F32)
    mixed_out = (own_tokens + (out_keep + tied(out_far, sent).astype(F32)) + bias_dense + bias_fc2).astype(BF)
    a_own, vec = summed(a_own, tied(a_got, mixed_out, fc1_grad), vec)
    a_grad = lax.reduce_precision(far_sum(a_own + far[None, :96].astype(F32)), 8, 7).astype(BF).reshape(96, width)
    a_got = exchange([a_grad] * 3)
    packet = exact(tied(vec, a_grad))
    vec = far_sum_exact(joined(packet) + joined(swap(packet, "dp", 1)))
    quarter_vec = vec + joined(far[96:])
    packet = exact(vec)
    vec = joined(packet) + joined(swap(packet, "tensor", 2))

    mine = jnp.stack(tied([a_grad, *a_got], vec))
    qkv_grad, dense_grad = finish(1, bits, mine, swap(mine, "dp", 1))
    e_far = tied(e_far, mine)

    e = e_keep + e_far.astype(F32)
    centered = own_tokens - jnp.mean(own_tokens, axis=-1, keepdims=True)
    r = lax.rsqrt(jnp.mean(centered * centered, axis=-1, keepdims=True) + EPS)
    xhat = centered * r
    dx = r * (e - jnp.mean(e, axis=-1, keepdims=True) - xhat * jnp.mean(e * xhat, axis=-1, keepdims=True))
    grad_tokens = (cotangent.astype(F32) + dx).astype(BF)

    columns = quarter_vec[1]
    return (
        mixed_out,
        grad_tokens,
        vec[2],
        vec[3],
        vec[4],
        vec[5],
        qkv_grad.reshape(3, 192, width).transpose(2, 0, 1),
        jnp.stack([columns[:192], columns[384:576]]),
        columns[192:384].reshape(3, 64)[:, :rot_dims],
        dense_grad,
        vec[6],
        fc1_grad,
        quarter_vec[0],
        fc2_grad,
        vec[6],
    )


def solution(mesh):
    rows = P(("dp", "tensor"), None)
    in_specs = (
        rows, rows, P(), P(), P(), P(), P(None, None, "tensor"), P(None, "tensor"), P("tensor", None),
        P("tensor", None), P(), P(None, "tensor"), P("tensor"), P("tensor", None), P(),
    )
    out_specs = (
        rows, rows, P(), P(), P(), P(), P(None, None, "tensor"), P(None, "tensor"), P("tensor", None),
        P("tensor", None), P(), P(None, "tensor"), P("tensor"), P("tensor", None), P(),
    )
    return jax.shard_map(body, mesh=mesh, in_specs=in_specs, out_specs=out_specs, check_vma=False)
```

```python
import math

import jax
import jax.numpy as jnp
from jax import lax
from jax.experimental import pallas as pl
from jax.experimental.pallas import tpu as pltpu
from jax.sharding import PartitionSpec as P

SEQ = 1024
EPS = 1e-05
BF = jnp.bfloat16
F32 = jnp.float32
BQ = 512
NB = SEQ // BQ
HALF = SEQ // 2


def nn(a, b):
    return lax.dot_general(a, b, (((1,), (0,)), ((), ())), preferred_element_type=F32)


def nt(a, b):
    return lax.dot_general(a, b, (((1,), (1,)), ((), ())), preferred_element_type=F32)


def call(kernel, name, args, outs, scratch=(), flops=0, transcendentals=0, limit=28):
    moved = sum(a.size * a.dtype.itemsize for a in args) + sum(math.prod(o[0]) * jnp.dtype(o[1]).itemsize for o in outs)
    spaces = [pltpu.SMEM if a.dtype == jnp.int32 else pltpu.VMEM for a in args]
    return pl.pallas_call(
        kernel,
        in_specs=[pl.BlockSpec(memory_space=s) for s in spaces],
        out_specs=[pl.BlockSpec(memory_space=pltpu.VMEM)] * len(outs),
        out_shape=[(pltpu.VMEM if stays else pltpu.HBM)(s, d) for s, d, stays in outs],
        scratch_shapes=[pltpu.VMEM(s, d) for s, d in scratch],
        compiler_params=pltpu.CompilerParams(vmem_limit_bytes=limit * 2**20),
        cost_estimate=pl.CostEstimate(flops=flops, bytes_accessed=moved, transcendentals=transcendentals),
        name=name,
    )(*args)


def near(values):
    return jax.tree.map(lambda v: pltpu.with_memory_space_constraint(v, pltpu.VMEM), values)


def away(values):
    return jax.tree.map(lambda v: pltpu.with_memory_space_constraint(v, pltpu.HBM), values)


def own_rows(bits_ref):
    half = bits_ref[1]
    return pl.ds(pl.multiple_of(HALF * half, HALF), HALF), pl.ds(pl.multiple_of(HALF - HALF * half, HALF), HALF)


def place_strips(bits_ref, mine, theirs, put):
    for slot in range(4):
        at = 96 * (bits_ref[2] ^ slot)
        put(pl.multiple_of(384 * bits_ref[0] + at, 96), mine[slot])
        put(pl.multiple_of(384 - 384 * bits_ref[0] + at, 96), theirs[slot])


def normalized(x_ref, gain, shift, put):
    for i in range(HALF // BQ):
        rows = pl.ds(i * BQ, BQ)
        x = x_ref[rows, :].astype(F32)
        centered = x - jnp.mean(x, axis=-1, keepdims=True)
        r = lax.rsqrt(jnp.mean(centered * centered, axis=-1, keepdims=True) + EPS)
        put(i * BQ, centered * r * gain + shift)


def tile(i):
    return slice(128 * i, 128 * (i + 1))


HEADS = ((0, 0, 1, 2, 0), (0, 1, 1, 2, 1), (4, 0, 5, 4, 1))
TILES = {0: (0, 64), 1: (192, 256), 2: (384, 448), 4: (128, 512), 5: (320, None)}
ROTATED = (0, 64, 128, 192, 256, 320)


def masked(x, half):
    keep = lax.broadcasted_iota(jnp.int32, x.shape, 1) < 64
    zero = jnp.zeros_like(x)
    return jnp.where(keep, x, zero) if half == 0 else jnp.where(keep, zero, x)


def causal(x, fill):
    rows = lax.broadcasted_iota(jnp.int32, x.shape, 0)
    cols = lax.broadcasted_iota(jnp.int32, x.shape, 1)
    return jnp.where(rows <= cols, x, fill)


def attn_forward_kernel(first, *refs):
    if first:
        bits_ref, x_ref, x_far_ref, norm_ref, w_ref, bias_ref, cos_ref, sin_ref = refs[:8]
        n_ref, qkv_ref, kt_ref, lse_ref, ot_ref, m_ref, o_ref, vt_ref = refs[8:]
        for x, at in ((x_ref, HALF * bits_ref[1]), (x_far_ref, HALF - HALF * bits_ref[1])):
            def put(row, n):
                n_ref[pl.ds(pl.multiple_of(at + row, BQ), BQ), :] = n.astype(BF)

            normalized(x, norm_ref[0:1], norm_ref[1:2], put)
    else:
        bits_ref, n_ref, w_ref, bias_ref, cos_ref, sin_ref, ot_in_ref, wd_in_ref, mlp_ref, mlp_far_ref = refs[:10]
        qkv_ref, kt_ref, lse_ref, ot_ref, keep_ref, send_ref, m_ref, o_ref, vt_ref, out_ref = refs[10:]
    n = n_ref[...]
    bias = bias_ref[...].T
    for at, size in ((0, 256), (256, 320)):
        m_ref[pl.ds(at, size), :] = nt(w_ref[pl.ds(at, size), :], n) + bias[at : at + size, 0:1]
    cos, sin = cos_ref[...], sin_ref[...]
    for at in ROTATED:
        one, two = m_ref[pl.ds(at, 8), :], m_ref[pl.ds(at + 8, 8), :]
        m_ref[pl.ds(at, 8), :] = one * cos - two * sin
        m_ref[pl.ds(at + 8, 8), :] = two * cos + one * sin
    m_ref[pl.ds(0, 192), :] = m_ref[pl.ds(0, 192), :] * 0.125
    for i, (one, two) in TILES.items():
        upper = jnp.zeros((64, SEQ), F32) if two is None else m_ref[pl.ds(two, 64), :]
        qkv_ref[:, tile(i)] = jnp.concatenate([m_ref[pl.ds(one, 64), :], upper], 0).T.astype(BF)
    kt_ref[...] = m_ref[pl.ds(192, 192), :].astype(BF)
    vt_ref[...] = m_ref[pl.ds(384, 192), :].astype(BF)

    lse_ref[...] = jnp.zeros((8, SEQ), F32)
    for h, (qt, qh, kt, vt, vh) in enumerate(HEADS):
        v_rows = pl.ds(64 * h, 64)
        for j in range(NB):
            cols = pl.ds(j * BQ, BQ)
            past = pl.ds(0, j * BQ)
            q = masked(qkv_ref[cols, tile(qt)], qh)
            st_d = causal(nt(qkv_ref[cols, tile(kt)], q), -1e30)
            top = jnp.max(st_d, axis=0, keepdims=True)
            if j:
                st = nt(qkv_ref[past, tile(kt)], q)
                top = jnp.maximum(top, jnp.max(st, axis=0, keepdims=True))
            w_d = jnp.exp(st_d - top)
            total = jnp.sum(w_d, axis=0, keepdims=True)
            o = nn(vt_ref[v_rows, cols], w_d.astype(BF))
            if j:
                w = jnp.exp(st - top)
                total = total + jnp.sum(w, axis=0, keepdims=True)
                o = o + nn(vt_ref[v_rows, past], w.astype(BF))
            o_ref[pl.ds(64 * h, 64), cols] = o * (1.0 / total)
            lse_ref[pl.ds(h, 1), cols] = top + jnp.log(total)
    ot_ref[...] = o_ref[...].astype(BF)
    if not first:
        own, far = own_rows(bits_ref)
        out_ref[...] = nn(o_ref[...].T.astype(BF), w_ref[pl.ds(576, 192), :]) + nn(
            ot_in_ref[...].astype(F32).T.astype(BF), wd_in_ref[...]
        )
        keep_ref[...] = out_ref[own, :] + mlp_ref[...].astype(F32)
        send_ref[...] = (out_ref[far, :] + mlp_far_ref[...].astype(F32)).astype(BF)


def attn_forward(first, *args):
    outs = [
        ((SEQ, 768), BF, False),
        ((SEQ, 768), BF, not first),
        ((192, SEQ), BF, not first),
        ((8, SEQ), F32, False),
        ((192, SEQ), BF, not first),
    ]
    scratch = [((576, SEQ), F32), ((192, SEQ), F32), ((192, SEQ), BF)]
    if not first:
        outs = outs[1:] + [((HALF, 768), F32, False), ((HALF, 768), BF, False)]
        scratch.append(((SEQ, 768), F32))
    kernel = lambda *refs: attn_forward_kernel(first, *refs)
    return call(kernel, "attn_forward", args, outs, scratch, 4 * 10**9, 2 * 10**6)


def normal_cdf(hidden):
    return 0.5 * (1.0 + lax.erf(hidden * math.sqrt(0.5)))


def mlp_hidden(n_ref, dy_ref, w1_ref, w2_ref, bias_ref, a_ref, dh_ref, db_ref):
    dy = dy_ref[...]
    for i in range(3):
        cols = slice(256 * i, 256 * (i + 1))
        hidden = nn(n_ref[...], w1_ref[:, cols]) + bias_ref[0:1, cols]
        cdf = normal_cdf(hidden)
        a_ref[:, cols] = (hidden * cdf).astype(BF)
        slope = cdf + hidden * (jnp.exp(-0.5 * hidden * hidden) * (1.0 / math.sqrt(2.0 * math.pi)))
        dh = (nt(dy, w2_ref[cols, :]) * slope).astype(BF)
        dh_ref[:, cols] = dh
        db_ref[:, cols] = jnp.broadcast_to(jnp.sum(dh.astype(F32), axis=0, keepdims=True), (8, 256))


def split_gradients(bits_ref, grads, keep_ref, send_ref):
    core = bits_ref[0]
    for i, g in enumerate(grads):
        keep_ref[i] = g[pl.ds(pl.multiple_of(384 * core, 384), 384), :].astype(BF)
        send_ref[i] = g[pl.ds(pl.multiple_of(384 - 384 * core, 384), 384), :].astype(BF)


def second_norm(x_ref, norm_ref, n_ref, nt_ref, at=0):
    def put(row, n):
        n_ref[pl.ds(at + row, BQ), :] = n.astype(BF)
        nt_ref[:, pl.ds(at + row, BQ)] = n.T.astype(BF)

    normalized(x_ref, norm_ref[2:3], norm_ref[3:4], put)


def mlp_half_kernel(first, *refs):
    if first:
        x_ref, norm_ref, dy_ref, w1_ref, w2_ref, bias_ref = refs[:6]
        out_ref, dn_ref, db_ref, g1_ref, g2_ref, n_ref, nt_ref, a_ref, dh_ref = refs[6:]
    else:
        x_ref, norm_ref, dy_ref, w1_ref, w2_ref, bias_ref, bits_ref, db_in_ref, g1_in_ref, g2_in_ref = refs[:10]
        out_ref, dn_ref, db_ref, keep_ref, send_ref, n_ref, nt_ref, a_ref, dh_ref, g1_ref, g2_ref = refs[10:]
    second_norm(x_ref, norm_ref, n_ref, nt_ref)
    mlp_hidden(n_ref, dy_ref, w1_ref, w2_ref, bias_ref, a_ref, dh_ref, db_ref)
    g1, g2 = nn(nt_ref[...], dh_ref[...]), nn(a_ref[...].T, dy_ref[...])
    g1_ref[...] = g1 if first else g1 + g1_in_ref[...]
    g2_ref[...] = g2 if first else g2 + g2_in_ref[...]
    out_ref[...] = nn(a_ref[...], w2_ref[...]).astype(BF)
    dn_ref[...] = nt(dh_ref[...], w1_ref[...]).astype(BF)
    if not first:
        db_ref[...] += db_in_ref[...]
        split_gradients(bits_ref, (g1_ref, g2_ref), keep_ref, send_ref)


SPLIT_OUTS = [((2, 384, 768), BF, False)] * 2


def mlp_half(first, *args):
    grads = [((768, 768), F32, True)] * 2
    outs = [((HALF, 768), BF, False)] * 2 + [((8, 768), F32, False)] + (grads if first else SPLIT_OUTS)
    scratch = [((HALF, 768), BF), ((768, HALF), BF), ((HALF, 768), BF), ((HALF, 768), BF)] + ([] if first else [g[:2] for g in grads])
    kernel = lambda *refs: mlp_half_kernel(first, *refs)
    return call(kernel, "mlp_half", args, outs, scratch, 36 * 10**8, 10**6)


def mlp_other_kernel(*refs):
    mine, theirs, refs = refs[:4], refs[4:8], refs[8:]
    bits_ref, bias_ref, norm_ref, x_ref, dy_ref, x_far_ref, dy_far_ref = refs[:7]
    refs = refs[7:]
    before, after = refs[:4], refs[4:8]
    db_ref, keep_ref, send_ref, wa_ref, n_ref, nt_ref, dy_all_ref, a_ref, dh_ref = refs[8:17]
    g1_ref, g2_ref, w1_ref, w2_ref = refs[17:]
    second_norm(x_ref, norm_ref, n_ref, nt_ref)
    second_norm(x_far_ref, norm_ref, n_ref, nt_ref, HALF)
    dy_all_ref[pl.ds(0, HALF), :] = dy_ref[...]
    dy_all_ref[pl.ds(HALF, HALF), :] = dy_far_ref[...]

    def put(row, ref):
        for i, w in enumerate((w1_ref, w2_ref, wa_ref)):
            w[pl.ds(row, 96), :] = ref[pl.ds(96 * i, 96), :]

    place_strips(bits_ref, mine, theirs, put)
    mlp_hidden(n_ref, dy_all_ref, w1_ref, w2_ref, bias_ref, a_ref, dh_ref, db_ref)
    g1_ref[...] = nn(nt_ref[...], dh_ref[...])
    g2_ref[...] = nn(a_ref[...].T, dy_all_ref[...])
    for half in range(2):
        rows = pl.ds(HALF * half, HALF)
        old, new = before[2 * half : 2 * half + 2], after[2 * half : 2 * half + 2]
        new[0][...] = (nn(a_ref[rows, :], w2_ref[...]) + old[0][...].astype(F32)).astype(BF)
        new[1][...] = (nt(dh_ref[rows, :], w1_ref[...]) + old[1][...].astype(F32)).astype(BF)
    split_gradients(bits_ref, (g1_ref, g2_ref), keep_ref, send_ref)


def mlp_other(*args):
    outs = [((HALF, 768), BF, False)] * 4
    outs += [((8, 768), F32, False)] + SPLIT_OUTS + [((768, 768), BF, False)]
    scratch = [((SEQ, 768), BF), ((768, SEQ), BF)] + [((SEQ, 768), BF)] * 3 + [((768, 768), F32)] * 2 + [((768, 768), BF)] * 2
    return call(mlp_other_kernel, "mlp_other", args, outs, scratch, 72 * 10**8, 2 * 10**6, 40)


def finish_kernel(kinds, bits_ref, *refs):
    mine, theirs = ([ref.at[slot] for slot in range(4)] for ref in refs[:2])
    outs = refs[2:]
    full = outs if kinds == 2 else outs[2:]

    def put(row, ref):
        for i, out in enumerate(full):
            out[pl.ds(row, 96), :] = ref[pl.ds(96 * i, 96), :].astype(F32)

    place_strips(bits_ref, mine, theirs, put)
    if kinds == 1:
        outs[0][...] = full[0][pl.ds(0, 576), :]
        outs[1][...] = full[0][pl.ds(576, 192), :]


def finish(kinds, bits, mine, theirs):
    shapes = [(768, 768), (768, 768)] if kinds == 2 else [(576, 768), (192, 768)]
    kernel = lambda *refs: finish_kernel(kinds, *refs)
    scratch = [] if kinds == 2 else [((768, 768), F32)]
    return call(kernel, "finish", (bits, mine, theirs), [(s, F32, False) for s in shapes], scratch)


def attn_backward_kernel(last, *refs):
    bits_ref, qkv_ref, kt_ref, lse_ref, ot_ref, n_ref, dy_own_ref, dy_far_ref, w_ref, cos_ref, sin_ref, db_ref = refs[:12]
    if last:
        in_ref, dn2_ref, dn2_far_ref, x_ref, x_far_ref, norm_ref = refs[12:18]
        keep_ref, send_ref, e_keep_ref, e_send_ref, raw_ref = refs[18:23]
        dn_ref = refs[-8]
    else:
        keep_ref, send_ref, dn_ref = refs[12:15]
    dy_ref, do_ref, dk_ref, dv_ref, dt_ref, d_ref, g_ref = refs[-7:]
    own, far = own_rows(bits_ref)
    dy_ref[own, :] = dy_own_ref[...]
    dy_ref[far, :] = dy_far_ref[...]
    dy = dy_ref[...]
    do_ref[0] = nt(dy, w_ref[pl.ds(576, 128), :]).astype(BF)
    do_ref[1] = nt(dy, w_ref[pl.ds(640, 128), :]).astype(BF)
    dk_ref[...] = jnp.zeros_like(dk_ref)
    dv_ref[...] = jnp.zeros_like(dv_ref)
    for h, (qt, qh, kt, vt, vh) in enumerate(HEADS):
        a = h // 2
        rows = pl.ds(64 * h, 64)
        for j in range(NB):
            cols = pl.ds(j * BQ, BQ)
            past = pl.ds(0, j * BQ)
            q = masked(qkv_ref[cols, tile(qt)], qh)
            do = masked(do_ref[a, cols, :], vh)
            lse = lse_ref[pl.ds(h, 1), cols]
            p_d = jnp.exp(causal(nt(qkv_ref[cols, tile(kt)], q), -1e30) - lse)
            dp_d = nt(qkv_ref[cols, tile(vt)], do)
            delta = jnp.sum(p_d * dp_d, axis=0, keepdims=True)
            if j:
                p = jnp.exp(nt(qkv_ref[past, tile(kt)], q) - lse)
                dp = nt(qkv_ref[past, tile(vt)], do)
                delta = delta + jnp.sum(p * dp, axis=0, keepdims=True)
            ds_d = (p_d * (dp_d - delta)).astype(BF)
            dv_ref[a, cols, :] += nn(p_d.astype(BF), do)
            dk_ref[a, cols, :] += nn(ds_d, q)
            dqt = nn(kt_ref[rows, cols], ds_d)
            if j:
                ds = (p * (dp - delta)).astype(BF)
                dv_ref[a, past, :] += nn(p.astype(BF), do)
                dk_ref[a, past, :] += nn(ds, q)
                dqt = dqt + nn(kt_ref[rows, past], ds)
            dt_ref[rows, cols] = dqt * 0.125
    dt_ref[pl.ds(192, 128), :] = dk_ref[0].T
    dt_ref[pl.ds(320, 64), :] = dk_ref[1].T[:64]
    dt_ref[pl.ds(384, 128), :] = dv_ref[0].T
    dt_ref[pl.ds(512, 64), :] = dv_ref[1].T[64:]
    dt_ref[pl.ds(576, 64), :] = jnp.zeros((64, SEQ), F32)
    cos, sin = cos_ref[...], sin_ref[...]
    for at in ROTATED:
        one, two = dt_ref[pl.ds(at, 8), :], dt_ref[pl.ds(at + 8, 8), :]
        dt_ref[pl.ds(at, 8), :] = one * cos + two * sin
        dt_ref[pl.ds(at + 8, 8), :] = two * cos - one * sin
    for i in range(5):
        d_ref[:, tile(i)] = dt_ref[tile(i), :].T.astype(BF)
    d = d_ref[...]
    g_ref[pl.ds(0, 576), :] = nn(dt_ref[pl.ds(0, 576), :].astype(BF), n_ref[...])
    g_ref[pl.ds(576, 192), :] = nn(ot_ref[...], dy)
    dn = nn(d, w_ref[pl.ds(0, 640), :])

    core = bits_ref[0]
    keep_ref[...] = g_ref[pl.ds(pl.multiple_of(384 * core, 384), 384), :].astype(BF)
    send_ref[pl.ds(0, 384), :] = g_ref[pl.ds(pl.multiple_of(384 - 384 * core, 384), 384), :].astype(BF)
    row = lax.broadcasted_iota(jnp.int32, (8, 768), 0)
    columns = jnp.concatenate([nn(jnp.ones((8, SEQ), BF), d), jnp.zeros((8, 128), F32)], 1)
    vec = jnp.where(row == 0, db_ref[...], jnp.where(row == 1, columns, 0.0))
    if last:
        dn_ref[...] = dn + in_ref[...]
        gain1, gain2 = norm_ref[0:1], norm_ref[2:3]
        sums = [0.0] * 4
        for rows, dn2_rows, x_rows in ((own, dn2_ref, x_ref), (far, dn2_far_ref, x_far_ref)):
            dn1, dn2, x = dn_ref[rows, :], dn2_rows[...].astype(F32), x_rows[...].astype(F32)
            e = dn1 * gain1 + dn2 * gain2
            if rows is own:
                e_keep_ref[...] = e
            else:
                e_send_ref[...] = e.astype(BF)
            centered = x - jnp.mean(x, axis=-1, keepdims=True)
            xhat = centered * lax.rsqrt(jnp.mean(centered * centered, axis=-1, keepdims=True) + EPS)
            for i, term in enumerate((dn1 * xhat, dn1, dn2 * xhat, dn2)):
                sums[i] = sums[i] + jnp.sum(term, axis=0, keepdims=True)
        sums.append(jnp.sum(dy_own_ref[...].astype(F32), axis=0, keepdims=True))
        for i, value in enumerate(sums):
            vec = jnp.where(row == 2 + i, value, vec)
    else:
        dn_ref[...] = dn
    high = vec.astype(BF)
    raw = jnp.concatenate([high, (vec - high.astype(F32)).astype(BF)], 0)
    send_ref[pl.ds(384, 16), :] = raw
    if last:
        raw_ref[...] = raw


def attn_backward(last, *args):
    outs = [((384, 768), BF, False), ((400, 768), BF, False)]
    if last:
        outs += [((HALF, 768), F32, False), ((HALF, 768), BF, False), ((16, 768), BF, False)]
    else:
        outs += [((SEQ, 768), F32, True)]
    scratch = [
        ((SEQ, 768), BF),
        ((2, SEQ, 128), BF),
        ((2, SEQ, 128), F32),
        ((2, SEQ, 128), F32),
        ((640, SEQ), F32),
        ((SEQ, 640), BF),
        ((768, 768), F32),
    ]
    if last:
        scratch.insert(0, ((SEQ, 768), F32))
    kernel = lambda *refs: attn_backward_kernel(last, *refs)
    return call(kernel, "attn_backward", args, outs, scratch, 5 * 10**9, 10**6, 40)


def swap(value, axis, distance):
    size = lax.axis_size(axis)
    return lax.ppermute(value, axis, [(i, i ^ distance) for i in range(size)])


def bit_of(axis, distance):
    return (lax.axis_index(axis) // distance) % 2


def exact(vec):
    high = lax.reduce_precision(vec, 8, 7)
    return jnp.concatenate([high.astype(BF), (vec - high).astype(BF)], 0)


def joined(pair):
    rows = pair.shape[0] // 2
    return pair[:rows].astype(F32) + pair[rows:].astype(F32)


def spot():
    return 2 * bit_of("dp", 2) + bit_of("dp", 4)


PEERS = ((4, 1), (2, 2), (6, 3))


def messages(keep, got, vec=None):
    def part(change):
        at = (spot() ^ change) * 96
        cut = lambda v: lax.dynamic_slice_in_dim(v, at, 96, 1).astype(F32)
        return cut(keep) + cut(got)

    out = []
    for _, change in PEERS:
        sent = part(change).astype(BF).reshape(-1, keep.shape[-1])
        out.append(sent if vec is None else jnp.concatenate([sent, exact(vec)], 0))
    return part(0), out


def exchange(out):
    return [swap(message, "dp", distance) for (distance, _), message in zip(PEERS, out)]


def summed(own, got, vec=None):
    rows = own.shape[0] * 96
    total = own
    for message in got:
        total = total + message[:rows].reshape(own.shape).astype(F32)
    if vec is None:
        return total
    y, x, both = (joined(message[rows:]) for message in got)
    return total, (joined(exact(vec)) + y) + (x + both)


def core_swap(parts):
    return [swap(part, "dp", 1) for part in parts]


def far_sum(value):
    distance = 8
    while distance < lax.axis_size("dp"):
        mine = lax.reduce_precision(value, 8, 7)
        value = mine + swap(mine.astype(BF), "dp", distance).astype(F32)
        distance *= 2
    return value


def far_sum_exact(vec):
    distance = 8
    while distance < lax.axis_size("dp"):
        mine = exact(vec)
        vec = joined(mine) + joined(swap(mine, "dp", distance))
        distance *= 2
    return vec


def rotary_tables(rot_dims):
    position = jnp.arange(SEQ).astype(F32)
    inverse = 1.0 / 10000.0 ** (jnp.arange(0, rot_dims, 2).astype(F32) / rot_dims)
    angles = inverse[:, None] * position[None, :]
    return jnp.cos(angles), jnp.sin(angles)


def tied(values, *others):
    return lax.optimization_barrier((values, others))[0]


def body(
    tokens, cotangent, attention_norm_gain, attention_norm_bias, feedforward_norm_gain, feedforward_norm_bias,
    w_qkv, bias_qv, bias_key, w_dense, bias_dense, w_fc1, bias_fc1, w_fc2, bias_fc2,
):
    width = tokens.shape[1]
    rot_dims = bias_key.shape[1]
    core = bit_of("dp", 1)
    bits = jnp.stack([core, bit_of("tensor", 1), spot()]).astype(jnp.int32)

    x_far = swap(tokens, "tensor", 1)

    wa = jnp.concatenate([w_qkv.transpose(1, 2, 0).reshape(-1, width), w_dense], 0)
    key_bias = jnp.pad(bias_key, ((0, 0), (0, 64 - rot_dims))).reshape(192)
    bias = jnp.stack([jnp.concatenate([bias_qv[0], key_bias, bias_qv[1], jnp.zeros((192,), F32)]), bias_fc1])
    at = (4 * core + spot()) * 96
    pieces = jnp.concatenate([lax.dynamic_slice_in_dim(w, at, 96, 0) for w in (w_fc1, w_fc2, wa)], 0)
    pieces_far = swap(pieces, "tensor", 2)
    bias_far = swap(bias, "tensor", 2)
    rotary = rotary_tables(rot_dims)
    pad8 = lambda row: jnp.broadcast_to(row[None], (8, width))
    norms = jnp.stack([attention_norm_gain, attention_norm_bias, feedforward_norm_gain, feedforward_norm_bias])

    b1 = pad8(bias[1])
    mlp_out, dn2, db, g1, g2 = mlp_half(True, tokens, norms, cotangent, w_fc1, w_fc2, b1)
    x_far = tied(x_far, g1)
    dy_far = swap(tied(cotangent, x_far), "tensor", 1)

    pieces_far = tied(pieces_far, x_far)
    x_far, bias_far = tied((x_far, bias_far), pieces_far, bias_far)
    got = exchange([pieces_far] * 3)
    n1, *saved, ot = attn_forward(True, bits, tokens, x_far, norms, wa, pad8(bias[0]), *rotary)
    dy_far, ot = tied((dy_far, ot), dy_far)
    mlp_out_far, dn2_far, db, keep, send = mlp_half(
        False, tied(x_far, ot), norms, dy_far, w_fc1, w_fc2, b1, bits, db, *near((g1, g2))
    )
    keep, send, got = tied((keep, send, got), got)
    send_far = swap(send, "dp", 1)
    mine = [pieces_far, *got]
    theirs = core_swap(mine)
    keep_own, send_own_far = keep, send_far

    mlp_out, dn2, mlp_out_far, dn2_far, db_far, keep, send, wa_far = mlp_other(
        *mine, *theirs, bits, pad8(bias_far[1]), norms, tokens, cotangent, x_far, dy_far,
        *away((mlp_out, tied(dn2, send_own_far), mlp_out_far, dn2_far)),
    )
    send_far = swap(send, "dp", 1)
    fc_far, sent = messages(keep, send_far)
    got = exchange(sent)
    n1, wa_far, ot = away((n1, tied(wa_far, sent), ot))
    *saved_far, out_keep, out_send = attn_forward(
        False, bits, n1, wa_far, pad8(bias_far[0]), *rotary, ot, w_dense, *away((mlp_out, mlp_out_far)),
    )
    out_send, saved_far, got = tied((out_send, saved_far, got), got)
    fc_far = summed(fc_far, got).astype(BF)
    fc_far_in = swap(fc_far, "tensor", 2)
    out_far = swap(tied(out_send, fc_far), "tensor", 1)
    fc_own, sent = messages(tied(keep_own, got), send_own_far)
    fc_got = exchange(sent)
    qkv, kt, lse, ot_far = tied(saved_far, fc_far, sent)
    keep, send, dn1 = attn_backward(
        False, bits, near(qkv), near(kt), lse, near(ot_far), n1, cotangent, dy_far, wa_far, *rotary, db_far
    )
    keep, send, dn1, fc_far_in, fc_got = tied((keep, send, dn1, fc_far_in, fc_got), fc_far_in, fc_got)
    send_far = swap(send, "dp", 1)
    vec_far = joined(send[384:]) + joined(send_far[384:])
    a_far, sent = messages(keep[None], send_far[None, :384], vec_far)
    fc_own = summed(fc_own, fc_got)
    fc_grad = lax.reduce_precision(far_sum(fc_own + fc_far_in.astype(F32)), 8, 7).astype(BF).reshape(192, width)
    sent = [jnp.concatenate([message, fc_grad], 0) for message in sent]
    got = exchange(sent)
    keep, send, e_keep, e_send, vec_raw = attn_backward(
        True, bits, *away((*saved, ot)), n1, cotangent, dy_far, wa, *rotary, db, near(tied(dn1, sent)),
        *away((dn2, dn2_far)), tokens, x_far, norms,
    )
    keep, send, e_keep, e_send, vec_raw, got, out_far = tied(
        (keep, send, e_keep, e_send, vec_raw, got, out_far), got, out_far
    )

    send_far = swap(send, "dp", 1)
    vec_pair = swap(vec_raw, "tensor", 1)
    fc_mine = jnp.stack([fc_grad, *(message[112:] for message in got)])
    fc_theirs = swap(fc_mine, "dp", 1)
    a_far, vec_far = summed(a_far, [message[:112] for message in got], vec_far)
    far_send = jnp.concatenate([a_far[0].astype(BF), exact(vec_far)], 0)
    far = swap(far_send, "tensor", 2)
    e_far = swap(e_send, "tensor", 1)
    shared = lax.broadcasted_iota(jnp.int32, (8, 1), 0) >= 2
    vec = joined(vec_raw) + jnp.where(shared, joined(vec_pair), 0.0)
    keep = tied(keep, fc_theirs, vec_pair)
    a_own, sent = messages(keep[None], send_far[None, :384], vec)
    a_got = exchange(sent)
    fc1_grad, fc2_grad = finish(2, bits, fc_mine, tied(fc_theirs, sent))
    own_tokens = tokens.astype(F32)
    mixed_out = (own_tokens + (out_keep + tied(out_far, sent).astype(F32)) + bias_dense + bias_fc2).astype(BF)
    a_own, vec = summed(a_own, tied(a_got, mixed_out, fc1_grad), vec)
    a_grad = lax.reduce_precision(far_sum(a_own + far[None, :96].astype(F32)), 8, 7).astype(BF).reshape(96, width)
    a_got = exchange([a_grad] * 3)
    packet = exact(tied(vec, a_grad))
    vec = far_sum_exact(joined(packet) + joined(swap(packet, "dp", 1)))
    quarter_vec = vec + joined(far[96:])
    packet = exact(vec)
    vec = joined(packet) + joined(swap(packet, "tensor", 2))

    mine = jnp.stack(tied([a_grad, *a_got], vec))
    qkv_grad, dense_grad = finish(1, bits, mine, swap(mine, "dp", 1))
    e_far = tied(e_far, mine)

    e = e_keep + e_far.astype(F32)
    centered = own_tokens - jnp.mean(own_tokens, axis=-1, keepdims=True)
    r = lax.rsqrt(jnp.mean(centered * centered, axis=-1, keepdims=True) + EPS)
    xhat = centered * r
    dx = r * (e - jnp.mean(e, axis=-1, keepdims=True) - xhat * jnp.mean(e * xhat, axis=-1, keepdims=True))
    grad_tokens = (cotangent.astype(F32) + dx).astype(BF)

    columns = quarter_vec[1]
    return (
        mixed_out,
        grad_tokens,
        vec[2],
        vec[3],
        vec[4],
        vec[5],
        qkv_grad.reshape(3, 192, width).transpose(2, 0, 1),
        jnp.stack([columns[:192], columns[384:576]]),
        columns[192:384].reshape(3, 64)[:, :rot_dims],
        dense_grad,
        vec[6],
        fc1_grad,
        quarter_vec[0],
        fc2_grad,
        vec[6],
    )


def solution(mesh):
    rows = P(("dp", "tensor"), None)
    in_specs = (
        rows, rows, P(), P(), P(), P(), P(None, None, "tensor"), P(None, "tensor"), P("tensor", None),
        P("tensor", None), P(), P(None, "tensor"), P("tensor"), P("tensor", None), P(),
    )
    out_specs = (
        rows, rows, P(), P(), P(), P(), P(None, None, "tensor"), P(None, "tensor"), P("tensor", None),
        P("tensor", None), P(), P(None, "tensor"), P("tensor"), P("tensor", None), P(),
    )
    return jax.shard_map(body, mesh=mesh, in_specs=in_specs, out_specs=out_specs, check_vma=False)
```
